256 devices in a mesh: expert: 64 (over z, x, core), hid: 4 (over y).
Axes of the slice: x: 4, y: 4, z: 8, core: 2. Of those that a mesh axis runs over, the one named last changes fastest.
Arguments:
- tokens: bfloat16 [8192, 2048], P('expert'), may hold values from -6 to 6
- logits: float32 [8192, 8], P('expert'), may hold values from -6 to 6
- expert_ids: int32 [8192, 8], P('expert'), may hold values from 0 to 127, all different within a row; in each aligned block of 128 rows (0 to 127, 128 to 255, ...) at most 12 rows name the same one
- gate_weight: bfloat16 [128, 768, 2048], P('expert', 'hid'), may hold values from -0.125 to 0.125
- up_weight: bfloat16 [128, 768, 2048], P('expert', 'hid'), may hold values from -0.125 to 0.125
- down_weight: bfloat16 [128, 768, 2048], P('expert', 'hid'), may hold values from -0.21875 to 0.21875
- grad_out: bfloat16 [8192, 2048], P('expert', 'hid'), may hold values from -6 to 6
Outputs:
- layer_out: bfloat16 [8192, 2048], P('expert', 'hid')
- grad_tokens: bfloat16 [8192, 2048], P('expert', 'hid')
- grad_logits: float32 [8192, 8], P('expert')
- grad_gate: bfloat16 [128, 768, 2048], P('expert', 'hid')
- grad_up: bfloat16 [128, 768, 2048], P('expert', 'hid')
- grad_down: bfloat16 [128, 768, 2048], P('expert', 'hid')
The draws below stay inside these ranges and needn't reach their ends.
Inputs may be any that keep to these rules, and one draw needn't show every extreme that they name: `expert_ids`: each token names 8 different experts. Among the tokens of one index of expert (aligned blocks of 128 tokens) no expert is named more than 12 times, a bound that some block reaches.
All inputs are finite; a program needn't handle non-finite values.
Results may differ from the reference program's by a relative error of at most 0.015.
Values may be sent and summed in bfloat16 or wider, within the bound.
A program may use at most 128 MiB of HBM per device.

```python
import math
import jax
import jax.numpy as jnp
import numpy as np
from jax import lax

D = 2048
FF = 768
TOP = 8
TOK_DEV = 128
EXPERTS = 128
TOKENS = 8192
CAP = 12
N_EXPERT = 64
N_HID = 4


def shard_levels(own_key, dims, pieces, low, high):
    def one(dim, parts):
        heights = jax.random.uniform(jax.random.fold_in(jax.random.fold_in(own_key, 6), dim), (parts,), jnp.float32, low / len(pieces), high / len(pieces))
        return jnp.repeat(jnp.exp(heights), dims[dim] // parts).reshape((-1,) + (1,) * (len(dims) - dim - 1))

    loudness = one(*pieces[0])
    for cut in pieces[1:]:
        loudness = loudness * one(*cut)
    return loudness


def deal_out(key, own, number, rows, number_of, top, reach, lean):
    order = jax.random.permutation(key, number_of)
    crowded, ordinary = load_shares(number_of, rows * top, reach, lean, True), load_shares(number_of, rows * top, reach, lean, False)
    places = jnp.arange(number_of)

    def named(sizes, turn):
        used = int((sizes > 0).sum())
        fixed = max(1, used // 4)
        passed = fixed + (places - fixed + turn * (used - fixed)) % max(1, number_of - fixed)
        return jnp.zeros((number_of,), jnp.int32).at[order[jnp.where(places < fixed, places, passed)]].set(jnp.asarray(sizes, jnp.int32))

    sizes = jnp.where(number % 4 == 0, named(crowded, number // 4), named(ordinary, number - number // 4 - 1))
    mixed = jax.random.permutation(jax.random.fold_in(own, 3), number_of)
    source_of, receiver = mixed[0:number_of // 2 * 2:2], mixed[1:number_of // 2 * 2:2]
    margin = jnp.minimum(sizes[source_of] - 1, reach - sizes[receiver]) // 2
    margin = jnp.where((source_of == order[0]) | (receiver == order[0]) | (sizes[receiver] == 0), 0, jnp.maximum(margin, 0))
    passed = jax.random.randint(jax.random.fold_in(own, 4), (number_of // 2,), 0, 1 << 20) % (margin + 1)
    sizes = sizes.at[source_of].add(-passed).at[receiver].add(passed)
    labels = jnp.searchsorted(jnp.cumsum(sizes), jnp.arange(rows * top), side="right").astype(jnp.int32)
    table = labels.reshape(top, rows).T
    table = table[jax.random.permutation(jax.random.fold_in(own, 1), rows)]
    turn = jax.random.randint(jax.random.fold_in(own, 2), (rows, 1), 0, top)
    return jnp.take_along_axis(table, (jnp.arange(top)[None, :] + turn) % top, axis=1)


def load_shares(count, total, bound, skew, full):
    portions = [(1 << 20) // math.isqrt(rank ** skew) + 1 for rank in range(1, count + 1)]
    largest = bound if full else min(bound, max(-(-total // count), total * portions[0] // sum(portions)))
    least = 1 if total - largest >= count - 1 else 0
    counts, spare = [largest] + [least] * (count - 1), total - largest - least * (count - 1)
    while spare > 0:
        movable = [i for i in range(1, count) if counts[i] < largest] or [i for i in range(1, count) if counts[i] < bound]
        mass, remaining = sum([portions[i] for i in movable]), spare
        for i in movable:
            extra = min(bound - counts[i], max(1, remaining * portions[i] // mass), spare)
            counts[i] = counts[i] + extra
            spare = spare - extra
    return np.array(counts)


def bell_draw(own_key, dims, width, limit, pieces=(), kind=jnp.bfloat16):
    factor_of = shard_levels(own_key, dims, pieces, -0.22, 0.18) if pieces else 1.0
    drawn = jax.random.normal(own_key, dims, jnp.float32) * width * factor_of
    return jnp.minimum(jnp.maximum(drawn, -limit), limit).astype(kind)


def setup_inputs(seed: int = 0) -> dict:
    splits = jax.random.split(jax.random.key(seed), 8)
    tokens = bell_draw(splits[0], (TOKENS, D), 1.0, 6.0, ((0, 64),))
    logits = bell_draw(splits[1], (TOKENS, TOP), 1.5, 6.0, ((0, 64),), jnp.float32)
    expert_ids_keys = jax.random.split(jax.random.fold_in(splits[2], 1), TOKENS // TOK_DEV)
    expert_ids_turns = jax.random.permutation(jax.random.fold_in(splits[2], 3), TOKENS // TOK_DEV)
    expert_ids = jax.vmap(lambda own, number: deal_out(jax.random.fold_in(splits[2], 2), own, number, TOK_DEV, EXPERTS, TOP, CAP, 0))(expert_ids_keys, expert_ids_turns).reshape((TOKENS, TOP))
    gate_weight = bell_draw(splits[3], (EXPERTS, FF, D), D ** -0.5, 0.125, ((0, 64), (1, 4)))
    up_weight = bell_draw(splits[4], (EXPERTS, FF, D), D ** -0.5, 0.125, ((0, 64), (1, 4)))
    down_weight = bell_draw(splits[5], (EXPERTS, FF, D), FF ** -0.5, 0.21875, ((0, 64), (1, 4)))
    grad_out = bell_draw(splits[6], (TOKENS, D), 1.0, 6.0, ((0, 64), (1, 4)))
    return {"tokens": tokens, "logits": logits, "expert_ids": expert_ids, "gate_weight": gate_weight, "up_weight": up_weight, "down_weight": down_weight, "grad_out": grad_out}


def reference(tokens, logits, expert_ids, gate_weight, up_weight, down_weight, grad_out):
    rows_all = TOKENS * TOP
    block_rows = TOK_DEV * TOP
    flat_ids = expert_ids.reshape(-1).astype(jnp.int32)
    one_hot = (flat_ids[:, None] == jnp.arange(EXPERTS, dtype=jnp.int32)[None, :]).astype(jnp.int32)
    running = jnp.cumsum(one_hot.reshape(N_EXPERT, block_rows, EXPERTS), axis=1).reshape(rows_all, EXPERTS)
    position = jnp.sum((running - 1) * one_hot, axis=1).astype(jnp.int32)
    source = jnp.arange(rows_all, dtype=jnp.int32) // block_rows
    slot_index = (flat_ids * N_EXPERT + source) * CAP + position
    slot_row = jnp.full((EXPERTS * N_EXPERT * CAP,), -1, jnp.int32)
    slot_row = slot_row.at[slot_index].set(jnp.arange(rows_all, dtype=jnp.int32)).reshape(EXPERTS, N_EXPERT * CAP)
    exps = jnp.exp(logits.astype(jnp.float32))
    probs = exps / jnp.sum(exps, axis=-1, keepdims=True)
    prob_flat = probs.reshape(-1)
    part_units = FF // N_HID
    places = N_EXPERT * CAP

    def expert_step(carry, inputs):
        out_acc, dx_acc, dprob_acc = carry
        w_gate, w_up, w_down, rows = inputs
        valid = rows >= 0
        picked = jnp.maximum(rows, 0)
        token_index = picked // TOP
        mask = valid[:, None]
        x_rows = jnp.where(mask, tokens[token_index], jnp.zeros((), tokens.dtype))
        pre_gate = jnp.dot(x_rows, w_gate.T, preferred_element_type=jnp.float32)
        pre_up = jnp.dot(x_rows, w_up.T, preferred_element_type=jnp.float32)
        sig_gate = jax.nn.sigmoid(pre_gate)
        activated = pre_gate * sig_gate
        hidden = (activated * pre_up).astype(jnp.bfloat16)
        partial_value = jnp.einsum('sgf,gfd->gsd', hidden.astype(jnp.float32).reshape(places, N_HID, part_units),
                             w_down.astype(jnp.float32).reshape(N_HID, part_units, D))
        partial_value = lax.optimization_barrier(partial_value.astype(jnp.bfloat16)).astype(jnp.float32)
        out_rows = jnp.sum(partial_value, axis=0).astype(jnp.bfloat16)
        prob_row = jnp.where(valid, prob_flat[picked], jnp.float32(0.0))
        out_acc = out_acc.at[token_index].add(prob_row[:, None] * out_rows.astype(jnp.float32))
        dy_rows = grad_out[token_index]
        dprob_rows = jnp.sum(dy_rows.astype(jnp.float32) * out_rows.astype(jnp.float32), axis=1)
        dprob_acc = dprob_acc.at[picked].add(jnp.where(valid, dprob_rows, jnp.float32(0.0)))
        grad_rows = (prob_row[:, None] * dy_rows.astype(jnp.float32)).astype(jnp.bfloat16)
        grad_hidden = jnp.dot(grad_rows, w_down.T, preferred_element_type=jnp.float32)
        grad_pre_gate = (grad_hidden * pre_up * sig_gate * (1.0 + pre_gate * (1.0 - sig_gate))).astype(jnp.bfloat16)
        grad_pre_up = (grad_hidden * activated).astype(jnp.bfloat16)
        grad_down_e = jnp.dot(hidden.T, grad_rows, preferred_element_type=jnp.float32).astype(jnp.bfloat16)
        grad_gate_e = jnp.dot(grad_pre_gate.T, x_rows, preferred_element_type=jnp.float32).astype(jnp.bfloat16)
        grad_up_e = jnp.dot(grad_pre_up.T, x_rows, preferred_element_type=jnp.float32).astype(jnp.bfloat16)
        back_part = jnp.einsum('sgf,gfd->gsd', grad_pre_gate.astype(jnp.float32).reshape(places, N_HID, part_units),
                               w_gate.astype(jnp.float32).reshape(N_HID, part_units, D))
        back_part = back_part + jnp.einsum('sgf,gfd->gsd', grad_pre_up.astype(jnp.float32).reshape(places, N_HID, part_units),
                                           w_up.astype(jnp.float32).reshape(N_HID, part_units, D))
        back_part = lax.optimization_barrier(back_part.astype(jnp.bfloat16)).astype(jnp.float32)
        grad_rows_in = jnp.sum(back_part, axis=0).astype(jnp.bfloat16)
        dx_acc = dx_acc.at[token_index].add(jnp.where(mask, grad_rows_in.astype(jnp.float32), jnp.float32(0.0)))
        return (out_acc, dx_acc, dprob_acc), (grad_gate_e, grad_up_e, grad_down_e)

    start = (jnp.zeros((TOKENS, D), jnp.float32), jnp.zeros((TOKENS, D), jnp.float32),
             jnp.zeros((rows_all,), jnp.float32))
    final, grads = lax.scan(expert_step, start, (gate_weight, up_weight, down_weight, slot_row))
    out_acc, dx_acc, dprob_acc = final
    grad_probs = dprob_acc.reshape(TOKENS, TOP)
    grad_logits = probs * (grad_probs - jnp.sum(probs * grad_probs, axis=-1, keepdims=True))
    return (out_acc.astype(jnp.bfloat16), dx_acc.astype(jnp.bfloat16), grad_logits,
            grads[0], grads[1], grads[2])
```

```python
import jax
import jax.numpy as jnp
from jax import lax
from jax.experimental import pallas as pl
from jax.experimental.pallas import tpu as pltpu
from jax.sharding import PartitionSpec as P

MESH = pl.DeviceIdType.MESH
F32, BF16 = jnp.float32, jnp.bfloat16
NZ, NJ, NY = 8, 8, 4
TOK, TOP, CAP, QW = 128, 8, 12, 512
ZHALF = 4
ROWS = ZHALF * CAP
EPL = 16
ORDER = (0, 1, -1, 2, -2, 3, -3, 4)


def dot_nt(a, b):
    return lax.dot_general(a, b, (((1,), (1,)), ((), ())), preferred_element_type=F32)


def dot_nn(a, b):
    return lax.dot_general(a, b, (((1,), (0,)), ((), ())), preferred_element_type=F32)


def dot_tn(a, b):
    return lax.dot_general(a, b, (((0,), (0,)), ((), ())), preferred_element_type=F32)


def kernel(
    tok, ids, logits, gw, uw, dw, go,
    layer_out, grad_tok, grad_log, ggate, gup, gdown,
    dense, ep, info, pick, prow, slots, rows, gwv, uwv, dwv, acts, part, rs_half, rs_left, rs_right,
    back, zsend, zback, dsend, dback, dy,
    zs, zr, xs, xr, ys, yr, dys, dyr, loc, own_sem,
):
    ex = lax.axis_index("expert")
    y = lax.axis_index("hid")
    z, j = lax.div(ex, NJ), lax.rem(ex, NJ)
    right, left, opp = lax.rem(y + 1, NY), lax.rem(y + 3, NY), lax.rem(y + 2, NY)

    def plane(i, sign):
        return lax.rem(z + sign * ORDER[i] + NZ, NZ)

    def mate(o, sign):
        return lax.rem(j + sign * o + NJ, NJ)

    loads = [
        pltpu.make_async_copy(tok.at[:, pl.ds(pl.multiple_of(y * QW, QW), QW)], dense.at[0, 0], loc.at[0]),
        pltpu.make_async_copy(go, dense.at[1, 0], loc.at[1]),
    ]
    wloads = [pltpu.make_async_copy(a, b, loc.at[2 + n]) for n, (a, b) in enumerate(((gw, gwv), (uw, uwv), (dw, dwv)))]
    for load in loads + wloads:
        load.start()

    barrier = pltpu.get_barrier_semaphore()
    for i in range(1, NZ):
        pl.semaphore_signal(barrier, inc=1, device_id=(plane(i, 1) * NJ + j, y), device_id_type=MESH)
    for o in range(1, NJ):
        pl.semaphore_signal(barrier, inc=1, device_id=(z * NJ + mate(o, 1), y), device_id_type=MESH)
    for h in (right, left, opp):
        pl.semaphore_signal(barrier, inc=1, device_id=(ex, h), device_id_type=MESH)

    exps = jnp.exp(logits[...])
    probs = exps / jnp.sum(exps, axis=0, keepdims=True)
    eio = lax.broadcasted_iota(jnp.int32, (TOK, TOK), 0)
    tio = lax.broadcasted_iota(jnp.int32, (TOK, TOK), 1)
    named = jnp.zeros((TOK, TOK), F32)
    weight = jnp.zeros((TOK, TOK), F32)
    for k in range(TOP):
        hit = eio == ids[k : k + 1, :]
        named = jnp.where(hit, 1.0, named)
        weight = jnp.where(hit, probs[k : k + 1, :], weight)
    earlier = dot_nn(named.astype(BF16), jnp.where(eio < tio, 1.0, 0.0).astype(BF16))
    ep[0] = jnp.where(named > 0.0, earlier, -1.0)
    ep[1] = weight
    info[0] = ep[:, pl.ds(pl.multiple_of(z * EPL, EPL), EPL), :]

    for load in loads:
        load.wait()
    pl.semaphore_wait(barrier, NZ + NJ + NY - 3)

    sent = []

    def send(src, dst, ssem, rsem, e, h):
        copy = pltpu.make_async_remote_copy(
            src_ref=src, dst_ref=dst, send_sem=ssem, recv_sem=rsem, device_id=(e, h), device_id_type=MESH
        )
        copy.start()
        sent.append(copy)

    def arrived(ref, ssem, rsem):
        pltpu.make_async_remote_copy(
            src_ref=ref, dst_ref=ref, send_sem=ssem, recv_sem=rsem, device_id=(ex, right), device_id_type=MESH
        ).wait_recv()

    for c in range(2):
        for a in range(2):
            for i in range(max(1, ZHALF * c), ZHALF * (c + 1)):
                zd = plane(i, -1)
                if a == 0:
                    send(ep.at[:, pl.ds(pl.multiple_of(zd * EPL, EPL), EPL), :], info.at[i],
                         zs.at[2, i], zr.at[2, i], zd * NJ + j, y)
                send(dense.at[a, 0], dense.at[a, i], zs.at[a, i], zr.at[a, i], zd * NJ + j, y)

    rio = lax.broadcasted_iota(jnp.int32, (ROWS, ZHALF * TOK), 0).astype(F32)

    def routes(c):
        span = range(ZHALF * c, ZHALF * (c + 1))
        for i in span:
            if i > 0:
                arrived(info.at[i], zs.at[2, i], zr.at[2, i])
        place = jnp.concatenate(
            [jnp.where(info[i, 0] >= 0.0, info[i, 0] + float(CAP * (i % ZHALF)), -1.0) for i in span], axis=1
        )
        share = jnp.concatenate([info[i, 1] for i in span], axis=1)
        for e in range(EPL):
            mask = rio == place[e : e + 1, :]
            pick[c, e * ROWS : (e + 1) * ROWS, :] = jnp.where(mask, 1.0, 0.0).astype(BF16)
            prow[c, e * ROWS : (e + 1) * ROWS, :] = jnp.sum(
                jnp.where(mask, share[e : e + 1, :], 0.0), axis=1, keepdims=True
            )

    own = {}

    def dispatch(a, c):
        for i in range(max(1, ZHALF * c), ZHALF * (c + 1)):
            arrived(dense.at[a, i], zs.at[a, i], zr.at[a, i])
        block = dense[a, ZHALF * c : ZHALF * (c + 1)].reshape(ZHALF * TOK, QW)
        placed = dot_nn(pick[c], block)
        if a == 1:
            placed = placed * prow[c]
        slots[a, c] = placed.astype(BF16).reshape(NJ, 2, ROWS, QW)
        mine = pl.ds(pl.multiple_of(j * ROWS, ROWS), ROWS)
        for o in range(1, NJ):
            jd = mate(o, 1)
            send(slots.at[a, c, jd], rows.at[a, y, c, :, mine, :],
                 xs.at[0, a, c, o], xr.at[0, a, c, o], z * NJ + jd, y)
        own[0, a, c] = pltpu.make_async_copy(slots.at[a, c, j], rows.at[a, y, c, :, mine, :], own_sem.at[0, a, c])
        own[0, a, c].start()

    def ring_send(a, c):
        for o in range(1, NJ):
            js = mate(o, -1)
            arrived(rows.at[a, y, c, :, pl.ds(pl.multiple_of(js * ROWS, ROWS), ROWS), :],
                    xs.at[0, a, c, o], xr.at[0, a, c, o])
        own[0, a, c].wait()
        for e in range(2):
            piece = rows.at[a, y, c, e]
            send(piece, piece, ys.at[0, a, c, e], yr.at[0, a, c, e], ex, right)
            piece = rows.at[a, y, c, 1 - e]
            send(piece, piece, ys.at[0, a, c, 3 - e], yr.at[0, a, c, 3 - e], ex, left)

    def ring_forward(a, c):
        arrived(rows.at[a, left, c, 0], ys.at[0, a, c, 0], yr.at[0, a, c, 0])
        piece = rows.at[a, left, c, 0]
        send(piece, piece, ys.at[0, a, c, 4], yr.at[0, a, c, 4], ex, right)
        arrived(rows.at[a, right, c, 1], ys.at[0, a, c, 3], yr.at[0, a, c, 3])
        piece = rows.at[a, right, c, 1]
        send(piece, piece, ys.at[0, a, c, 5], yr.at[0, a, c, 5], ex, left)

    def ring_end(a, c):
        for n, (src, e) in enumerate(((left, 0), (left, 1), (right, 0), (right, 1), (opp, 0), (opp, 1))):
            if n not in (0, 3):
                arrived(rows.at[a, src, c, e], ys.at[0, a, c, n], yr.at[0, a, c, n])

    def compute(c):
        def expert(e, carry):
            pre_gate = pre_up = grad_hidden = 0.0
            for q in range(NY):
                cols = slice(q * QW, (q + 1) * QW)
                x = rows[0, q, c, e]
                pre_gate += dot_nt(x, gwv[e, :, cols])
                pre_up += dot_nt(x, uwv[e, :, cols])
                grad_hidden += dot_nt(rows[1, q, c, e], dwv[e, :, cols])
            sig = jax.nn.sigmoid(pre_gate)
            act = pre_gate * sig
            hidden = act * pre_up
            gpg = grad_hidden * pre_up * sig * (1.0 + pre_gate * (1.0 - sig))
            gpu = grad_hidden * act
            acts[0, c, e] = hidden.T.astype(BF16)
            acts[1, c, e] = gpg.T.astype(BF16)
            acts[2, c, e] = gpu.T.astype(BF16)
            hidden, gpg, gpu = hidden.astype(BF16), gpg.astype(BF16), gpu.astype(BF16)
            for q in range(NY):
                cols = slice(q * QW, (q + 1) * QW)
                part[0, c, q, e] = dot_nn(hidden, dwv[e, :, cols]).astype(BF16)
                part[1, c, q, e] = (dot_nn(gpg, gwv[e, :, cols]) + dot_nn(gpu, uwv[e, :, cols])).astype(BF16)
            return carry

        lax.fori_loop(0, 2, expert, 0)

    def scatter_send(a, c):
        for dst, e, target, n, h in (
            (opp, 0, rs_half.at[a, c, 0], 0, right),
            (opp, 1, rs_half.at[a, c, 1], 1, left),
            (right, 1, rs_left.at[a, c, 1], 2, right),
            (left, 0, rs_right.at[a, c, 0], 3, left),
        ):
            send(part.at[a, c, dst, e], target, ys.at[1, a, c, n], yr.at[1, a, c, n], ex, h)

    def scatter_add(a, c):
        arrived(rs_half.at[a, c, 0], ys.at[1, a, c, 0], yr.at[1, a, c, 0])
        part[a, c, right, 0] = (part[a, c, right, 0].astype(F32) + rs_half[a, c, 0].astype(F32)).astype(BF16)
        send(part.at[a, c, right, 0], rs_left.at[a, c, 0], ys.at[1, a, c, 4], yr.at[1, a, c, 4], ex, right)
        arrived(rs_half.at[a, c, 1], ys.at[1, a, c, 1], yr.at[1, a, c, 1])
        part[a, c, left, 1] = (part[a, c, left, 1].astype(F32) + rs_half[a, c, 1].astype(F32)).astype(BF16)
        send(part.at[a, c, left, 1], rs_right.at[a, c, 1], ys.at[1, a, c, 5], yr.at[1, a, c, 5], ex, left)

    def scatter_end(a, c):
        for n, ref in ((2, rs_left.at[a, c, 1]), (3, rs_right.at[a, c, 0]),
                       (4, rs_left.at[a, c, 0]), (5, rs_right.at[a, c, 1])):
            arrived(ref, ys.at[1, a, c, n], yr.at[1, a, c, n])
        for e in range(2):
            part[a, c, y, e] = (part[a, c, y, e].astype(F32) + rs_left[a, c, e].astype(F32)
                                + rs_right[a, c, e].astype(F32)).astype(BF16)
        for o in range(1, NJ):
            jd = mate(o, 1)
            send(part.at[a, c, y, :, pl.ds(pl.multiple_of(jd * ROWS, ROWS), ROWS), :], back.at[a, c, j],
                 xs.at[1, a, c, o], xr.at[1, a, c, o], z * NJ + jd, y)
        own[1, a, c] = pltpu.make_async_copy(
            part.at[a, c, y, :, pl.ds(pl.multiple_of(j * ROWS, ROWS), ROWS), :], back.at[a, c, j], own_sem.at[1, a, c]
        )
        own[1, a, c].start()

    def combine(a, c):
        for o in range(1, NJ):
            js = mate(o, -1)
            arrived(back.at[a, c, js], xs.at[1, a, c, o], xr.at[1, a, c, o])
        own[1, a, c].wait()
        got = back[a, c].reshape(EPL * ROWS, QW)
        chosen = pick[c]
        span = slice(ZHALF * c, ZHALF * (c + 1))
        if a == 0:
            dots = dot_nt(got, dense[1, span].reshape(ZHALF * TOK, QW))
            dots = jnp.where(chosen > 0, dots, 0.0).reshape(EPL, ROWS, ZHALF * TOK)
            dots = jnp.sum(dots, axis=1)
            for i in range(ZHALF):
                dsend[ZHALF * c + i] = dots[:, i * TOK : (i + 1) * TOK]
            got = (got.astype(F32) * prow[c]).astype(BF16)
        zsend[a, span] = dot_tn(chosen, got).astype(BF16).reshape(ZHALF, TOK, QW)
        for i in range(ZHALF * c, ZHALF * (c + 1)):
            if i == 0:
                if a == 0:
                    dback[z] = dsend[0]
                continue
            zd = plane(i, 1)
            if a == 0:
                send(dsend.at[i], dback.at[z], zs.at[5, i], zr.at[5, i], zd * NJ + j, y)
            send(zsend.at[a, i], zback.at[a, i], zs.at[3 + a, i], zr.at[3 + a, i], zd * NJ + j, y)

    def finish(a, out):
        total = zsend[a, 0].astype(F32)
        for i in range(1, NZ):
            arrived(zback.at[a, i], zs.at[3 + a, i], zr.at[3 + a, i])
            total = total + zback[a, i].astype(F32)
        out[...] = total.astype(BF16)

    routes(0)
    dispatch(0, 0)
    dispatch(1, 0)
    ring_send(0, 0)
    routes(1)
    dispatch(0, 1)
    ring_send(1, 0)
    dispatch(1, 1)
    ring_forward(0, 0)
    ring_send(0, 1)
    ring_forward(1, 0)
    ring_send(1, 1)
    ring_end(0, 0)
    ring_end(1, 0)
    for load in wloads:
        load.wait()
    compute(0)
    ring_forward(0, 1)
    scatter_send(0, 0)
    ring_forward(1, 1)
    scatter_send(1, 0)
    ring_end(0, 1)
    ring_end(1, 1)
    compute(1)
    scatter_send(0, 1)
    scatter_send(1, 1)
    scatter_add(0, 0)
    scatter_add(1, 0)
    scatter_add(0, 1)
    scatter_add(1, 1)
    scatter_end(0, 0)

    def grads(e, carry):
        for q in range(NY):
            cols = slice(q * QW, (q + 1) * QW)
            for n, a, ref in ((0, 1, dwv), (1, 0, gwv), (2, 0, uwv)):
                ref[e, :, cols] = (dot_nn(acts[n, 0, e], rows[a, q, 0, e])
                                   + dot_nn(acts[n, 1, e], rows[a, q, 1, e])).astype(BF16)
        return carry

    lax.fori_loop(0, 2, grads, 0)
    stores = [pltpu.make_async_copy(a, b, loc.at[5 + n])
              for n, (a, b) in enumerate(((gwv, ggate), (uwv, gup), (dwv, gdown)))]
    for store in stores:
        store.start()

    combine(0, 0)
    scatter_end(0, 1)
    combine(0, 1)
    scatter_end(1, 0)
    combine(1, 0)
    scatter_end(1, 1)

    for i in range(1, NZ):
        zo = plane(i, -1)
        arrived(dback.at[zo], zs.at[5, i], zr.at[5, i])
    every = dback[...].reshape(TOK, TOK)
    for k in range(TOP):
        hit = eio == ids[k : k + 1, :]
        dy[0, k : k + 1, :] = jnp.sum(jnp.where(hit, every, 0.0), axis=0, keepdims=True)
    for n, h in ((1, right), (2, opp), (3, left)):
        send(dy.at[0], dy.at[n], dys.at[n], dyr.at[n], ex, h)
    finish(0, layer_out)
    combine(1, 1)
    for n in range(1, NY):
        arrived(dy.at[n], dys.at[n], dyr.at[n])
    grad_probs = dy[0] + dy[1] + dy[2] + dy[3]
    grad_log[...] = probs * (grad_probs - jnp.sum(probs * grad_probs, axis=0, keepdims=True))
    finish(1, grad_tok)

    for store in stores:
        store.wait()
    for copy in sent:
        copy.wait_send()


def body(tokens, logits, expert_ids, gate_weight, up_weight, down_weight, grad_out):
    any_spec = pl.BlockSpec(memory_space=pl.ANY)
    vmem = pl.BlockSpec(memory_space=pltpu.VMEM)
    half = ZHALF * CAP * NJ
    weight = jax.ShapeDtypeStruct(gate_weight.shape, BF16)
    quarter = jax.ShapeDtypeStruct((TOK, QW), BF16)
    layer_out, grad_tok, grad_log, ggate, gup, gdown = pl.pallas_call(
        kernel,
        out_shape=(quarter, quarter, jax.ShapeDtypeStruct((TOP, TOK), F32), weight, weight, weight),
        in_specs=[any_spec, vmem, vmem, any_spec, any_spec, any_spec, any_spec],
        out_specs=(vmem, vmem, vmem, any_spec, any_spec, any_spec),
        scratch_shapes=[
            pltpu.VMEM((2, NZ, TOK, QW), BF16),
            pltpu.VMEM((2, TOK, TOK), F32),
            pltpu.VMEM((NZ, 2, EPL, TOK), F32),
            pltpu.VMEM((2, EPL * ROWS, ZHALF * TOK), BF16),
            pltpu.VMEM((2, EPL * ROWS, 1), F32),
            pltpu.VMEM((2, 2, NJ, 2, ROWS, QW), BF16),
            pltpu.VMEM((2, NY, 2, 2, half, QW), BF16),
            pltpu.VMEM(gate_weight.shape, BF16),
            pltpu.VMEM(gate_weight.shape, BF16),
            pltpu.VMEM(gate_weight.shape, BF16),
            pltpu.VMEM((3, 2, 2, gate_weight.shape[1], half), BF16),
            pltpu.VMEM((2, 2, NY, 2, half, QW), BF16),
            pltpu.VMEM((2, 2, 2, half, QW), BF16),
            pltpu.VMEM((2, 2, 2, half, QW), BF16),
            pltpu.VMEM((2, 2, 2, half, QW), BF16),
            pltpu.VMEM((2, 2, NJ, 2, ROWS, QW), BF16),
            pltpu.VMEM((2, NZ, TOK, QW), BF16),
            pltpu.VMEM((2, NZ, TOK, QW), BF16),
            pltpu.VMEM((NZ, EPL, TOK), F32),
            pltpu.VMEM((NZ, EPL, TOK), F32),
            pltpu.VMEM((NY, TOP, TOK), F32),
            pltpu.SemaphoreType.DMA((6, NZ)),
            pltpu.SemaphoreType.DMA((6, NZ)),
            pltpu.SemaphoreType.DMA((2, 2, 2, NJ)),
            pltpu.SemaphoreType.DMA((2, 2, 2, NJ)),
            pltpu.SemaphoreType.DMA((2, 2, 2, 6)),
            pltpu.SemaphoreType.DMA((2, 2, 2, 6)),
            pltpu.SemaphoreType.DMA((NY,)),
            pltpu.SemaphoreType.DMA((NY,)),
            pltpu.SemaphoreType.DMA((8,)),
            pltpu.SemaphoreType.DMA((2, 2, 2)),
        ],
        compiler_params=pltpu.CompilerParams(
            collective_id=0, has_side_effects=True, vmem_limit_bytes=63 * 1024 * 1024
        ),
    )(tokens, expert_ids.T, logits.T, gate_weight, up_weight, down_weight, grad_out)
    return (layer_out, grad_tok, grad_log.T, ggate, gup, gdown)


def solution(mesh):
    placed = (
        P("expert", None),
        P("expert", None),
        P("expert", None),
        P("expert", "hid", None),
        P("expert", "hid", None),
        P("expert", "hid", None),
        P("expert", "hid"),
    )
    return jax.shard_map(
        body,
        mesh=mesh,
        in_specs=placed,
        out_specs=(
            P("expert", "hid"),
            P("expert", "hid"),
            P("expert", None),
            P("expert", "hid", None),
            P("expert", "hid", None),
            P("expert", "hid", None),
        ),
        check_vma=False,
    )
```

```python
import jax
import jax.numpy as jnp
from jax import lax
from jax.experimental import pallas as pl
from jax.experimental.pallas import tpu as pltpu
from jax.sharding import PartitionSpec as P

MESH = pl.DeviceIdType.MESH
F32, BF16 = jnp.float32, jnp.bfloat16
NZ, NJ, NY = 8, 8, 4
TOK, TOP, CAP, QW = 128, 8, 12, 512
ZHALF = 4
ROWS = ZHALF * CAP
EPL = 16
ORDER = (0, 1, -1, 2, -2, 3, -3, 4)


def dot_nt(a, b):
    return lax.dot_general(a, b, (((1,), (1,)), ((), ())), preferred_element_type=F32)


def dot_nn(a, b):
    return lax.dot_general(a, b, (((1,), (0,)), ((), ())), preferred_element_type=F32)


def dot_tn(a, b):
    return lax.dot_general(a, b, (((0,), (0,)), ((), ())), preferred_element_type=F32)


def kernel(
    tok, ids, logits, gw, uw, dw, go,
    layer_out, grad_tok, grad_log, ggate, gup, gdown,
    dense, densex, ep, info, pick, prow, slots, rows, gwv, uwv, dwv, acts, part, rs_half, rs_left, rs_right,
    back, zsend, zback, dsend, dback, dy,
    zs, zr, xs, xr, ys, yr, dys, dyr, loc, own_sem,
):
    ex = lax.axis_index("expert")
    y = lax.axis_index("hid")
    z, j = lax.div(ex, NJ), lax.rem(ex, NJ)
    right, left, opp = lax.rem(y + 1, NY), lax.rem(y + 3, NY), lax.rem(y + 2, NY)

    def plane(i, sign):
        return lax.rem(z + sign * ORDER[i] + NZ, NZ)

    def mate(o, sign):
        return lax.rem(j + sign * o + NJ, NJ)

    loads = [
        pltpu.make_async_copy(go, dense.at[0], loc.at[1]),
        pltpu.make_async_copy(tok, densex.at[0], loc.at[0]),
    ]
    wloads = [pltpu.make_async_copy(a, b, loc.at[2 + n]) for n, (a, b) in enumerate(((gw, gwv), (uw, uwv), (dw, dwv)))]
    for load in loads + wloads:
        load.start()

    barrier = pltpu.get_barrier_semaphore()
    for i in range(1, NZ):
        pl.semaphore_signal(barrier, inc=1, device_id=(plane(i, 1) * NJ + j, y), device_id_type=MESH)
    for o in range(1, NJ):
        pl.semaphore_signal(barrier, inc=1, device_id=(z * NJ + mate(o, 1), y), device_id_type=MESH)
    for h in (right, left, opp):
        pl.semaphore_signal(barrier, inc=1, device_id=(ex, h), device_id_type=MESH)

    exps = jnp.exp(logits[...])
    probs = exps / jnp.sum(exps, axis=0, keepdims=True)
    eio = lax.broadcasted_iota(jnp.int32, (TOK, TOK), 0)
    tio = lax.broadcasted_iota(jnp.int32, (TOK, TOK), 1)
    named = jnp.zeros((TOK, TOK), F32)
    weight = jnp.zeros((TOK, TOK), F32)
    for k in range(TOP):
        hit = eio == ids[k : k + 1, :]
        named = jnp.where(hit, 1.0, named)
        weight = jnp.where(hit, probs[k : k + 1, :], weight)
    earlier = dot_nn(named.astype(BF16), jnp.where(eio < tio, 1.0, 0.0).astype(BF16))
    ep[0] = jnp.where(named > 0.0, earlier, -1.0)
    ep[1] = weight
    info[0] = ep[:, pl.ds(pl.multiple_of(z * EPL, EPL), EPL), :]

    for load in loads:
        load.wait()
    pl.semaphore_wait(barrier, NZ + NJ + NY - 3)

    sent = []

    def send(src, dst, ssem, rsem, e, h):
        copy = pltpu.make_async_remote_copy(
            src_ref=src, dst_ref=dst, send_sem=ssem, recv_sem=rsem, device_id=(e, h), device_id_type=MESH
        )
        copy.start()
        sent.append(copy)

    def arrived(ref, ssem, rsem):
        pltpu.make_async_remote_copy(
            src_ref=ref, dst_ref=ref, send_sem=ssem, recv_sem=rsem, device_id=(ex, right), device_id_type=MESH
        ).wait_recv()

    def gather_piece(a, i, half):
        ref = (densex if a == 0 else dense).at[i]
        return ref if half is None else ref.at[half * (TOK // 2) : (half + 1) * (TOK // 2)]

    def gather_send(a, i):
        for n in ((1, 2) if i == 0 else (i + 2,)):
            down = n % 2 == 1 if i == 0 else i % 2 == 1
            half = None
            if n > 6:
                half, n = n - 7, 7
            src = gather_piece(a, i, half)
            sem = n if half is None else NZ - 1 + half
            send(src, gather_piece(a, n, half), zs.at[a, sem], zr.at[a, sem],
                 plane(1, -1 if down else 1) * NJ + j, y)

    def gather_wait(a, i):
        if i < NZ - 1:
            arrived(gather_piece(a, i, None), zs.at[a, i], zr.at[a, i])
        else:
            for half in range(2):
                arrived(gather_piece(a, i, half), zs.at[a, i + half], zr.at[a, i + half])

    for i in range(1, NZ):
        zd = plane(i, -1)
        send(ep.at[:, pl.ds(pl.multiple_of(zd * EPL, EPL), EPL), :], info.at[i],
             zs.at[2, i], zr.at[2, i], zd * NJ + j, y)

    rio = lax.broadcasted_iota(jnp.int32, (ROWS, ZHALF * TOK), 0).astype(F32)

    def routes(c):
        span = range(ZHALF * c, ZHALF * (c + 1))
        for i in span:
            if i > 0:
                arrived(info.at[i], zs.at[2, i], zr.at[2, i])
        place = jnp.concatenate(
            [jnp.where(info[i, 0] >= 0.0, info[i, 0] + float(CAP * (i % ZHALF)), -1.0) for i in span], axis=1
        )
        share = jnp.concatenate([info[i, 1] for i in span], axis=1)
        for e in range(EPL):
            first = (e % 2) * NJ * ROWS + (e // 2) * ROWS
            mask = rio == place[e : e + 1, :]
            pick[c, first : first + ROWS, :] = jnp.where(mask, 1.0, 0.0).astype(BF16)
            prow[c, first : first + ROWS, :] = jnp.sum(
                jnp.where(mask, share[e : e + 1, :], 0.0), axis=1, keepdims=True
            )

    own = {}

    def rows_of(d):
        return pl.ds(pl.multiple_of(d * ROWS, ROWS), ROWS)

    staged = {}

    def dispatch_tokens(c):
        span = slice(ZHALF * c, ZHALF * (c + 1))
        for q in range(NY):
            block = densex[span, :, q * QW : (q + 1) * QW].reshape(ZHALF * TOK, QW)
            part[1, c, q] = dot_nn(pick[c], block).astype(BF16).reshape(2, NJ * ROWS, QW)
        before = len(sent)
        for o in range(1, NJ):
            jd = mate(o, 1)
            send(part.at[1, c, :, :, rows_of(jd), :], rows.at[0, :, c, :, rows_of(j), :],
                 xs.at[0, 0, c, o], xr.at[0, 0, c, o], z * NJ + jd, y)
        staged[c] = sent[before:]
        del sent[before:]
        own[0, 0, c] = pltpu.make_async_copy(
            part.at[1, c, :, :, rows_of(j), :], rows.at[0, :, c, :, rows_of(j), :], own_sem.at[0, 0, c]
        )
        own[0, 0, c].start()

    def tokens_end(c):
        for o in range(1, NJ):
            js = mate(o, -1)
            arrived(rows.at[0, :, c, :, rows_of(js), :], xs.at[0, 0, c, o], xr.at[0, 0, c, o])
        own[0, 0, c].wait()
        for copy in staged[c]:
            copy.wait_send()

    def dispatch_cotangents(c):
        block = dense[ZHALF * c : ZHALF * (c + 1)].reshape(ZHALF * TOK, QW)
        slots[c] = (dot_nn(pick[c], block) * prow[c]).astype(BF16).reshape(2, NJ * ROWS, QW)
        for o in range(1, NJ):
            jd = mate(o, 1)
            send(slots.at[c, :, rows_of(jd), :], rows.at[1, y, c, :, rows_of(j), :],
                 xs.at[0, 1, c, o], xr.at[0, 1, c, o], z * NJ + jd, y)
        own[0, 1, c] = pltpu.make_async_copy(
            slots.at[c, :, rows_of(j), :], rows.at[1, y, c, :, rows_of(j), :], own_sem.at[0, 1, c]
        )
        own[0, 1, c].start()

    def ring_send(a, c):
        for o in range(1, NJ):
            js = mate(o, -1)
            arrived(rows.at[a, y, c, :, rows_of(js), :],
                    xs.at[0, a, c, o], xr.at[0, a, c, o])
        own[0, a, c].wait()
        for e in range(2):
            piece = rows.at[a, y, c, e]
            send(piece, piece, ys.at[0, a, c, e], yr.at[0, a, c, e], ex, right)
            piece = rows.at[a, y, c, 1 - e]
            send(piece, piece, ys.at[0, a, c, 3 - e], yr.at[0, a, c, 3 - e], ex, left)

    def ring_forward(a, c):
        arrived(rows.at[a, left, c, 0], ys.at[0, a, c, 0], yr.at[0, a, c, 0])
        piece = rows.at[a, left, c, 0]
        send(piece, piece, ys.at[0, a, c, 4], yr.at[0, a, c, 4], ex, right)
        arrived(rows.at[a, right, c, 1], ys.at[0, a, c, 3], yr.at[0, a, c, 3])
        piece = rows.at[a, right, c, 1]
        send(piece, piece, ys.at[0, a, c, 5], yr.at[0, a, c, 5], ex, left)

    def ring_end(a, c):
        for n, (src, e) in enumerate(((left, 0), (left, 1), (right, 0), (right, 1), (opp, 0), (opp, 1))):
            if n not in (0, 3):
                arrived(rows.at[a, src, c, e], ys.at[0, a, c, n], yr.at[0, a, c, n])

    def compute(c):
        def expert(e, carry):
            pre_gate = pre_up = grad_hidden = 0.0
            for q in range(NY):
                cols = slice(q * QW, (q + 1) * QW)
                x = rows[0, q, c, e]
                pre_gate += dot_nt(x, gwv[e, :, cols])
                pre_up += dot_nt(x, uwv[e, :, cols])
                grad_hidden += dot_nt(rows[1, q, c, e], dwv[e, :, cols])
            sig = jax.nn.sigmoid(pre_gate)
            act = pre_gate * sig
            hidden = act * pre_up
            gpg = grad_hidden * pre_up * sig * (1.0 + pre_gate * (1.0 - sig))
            gpu = grad_hidden * act
            acts[0, c, e] = hidden.T.astype(BF16)
            acts[1, c, e] = gpg.T.astype(BF16)
            acts[2, c, e] = gpu.T.astype(BF16)
            hidden, gpg, gpu = hidden.astype(BF16), gpg.astype(BF16), gpu.astype(BF16)
            for q in range(NY):
                cols = slice(q * QW, (q + 1) * QW)
                part[0, c, q, e] = dot_nn(hidden, dwv[e, :, cols]).astype(BF16)
                part[1, c, q, e] = (dot_nn(gpg, gwv[e, :, cols]) + dot_nn(gpu, uwv[e, :, cols])).astype(BF16)
            return carry

        lax.fori_loop(0, 2, expert, 0)

    def scatter_send(a, c):
        for dst, e, target, n, h in (
            (opp, 0, rs_half.at[a, c, 0], 0, right),
            (opp, 1, rs_half.at[a, c, 1], 1, left),
            (right, 1, rs_left.at[a, c, 1], 2, right),
            (left, 0, rs_right.at[a, c, 0], 3, left),
        ):
            send(part.at[a, c, dst, e], target, ys.at[1, a, c, n], yr.at[1, a, c, n], ex, h)

    def scatter_add(a, c):
        arrived(rs_half.at[a, c, 0], ys.at[1, a, c, 0], yr.at[1, a, c, 0])
        part[a, c, right, 0] = (part[a, c, right, 0].astype(F32) + rs_half[a, c, 0].astype(F32)).astype(BF16)
        send(part.at[a, c, right, 0], rs_left.at[a, c, 0], ys.at[1, a, c, 4], yr.at[1, a, c, 4], ex, right)
        arrived(rs_half.at[a, c, 1], ys.at[1, a, c, 1], yr.at[1, a, c, 1])
        part[a, c, left, 1] = (part[a, c, left, 1].astype(F32) + rs_half[a, c, 1].astype(F32)).astype(BF16)
        send(part.at[a, c, left, 1], rs_right.at[a, c, 1], ys.at[1, a, c, 5], yr.at[1, a, c, 5], ex, left)

    def scatter_end(a, c):
        for n, ref in ((2, rs_left.at[a, c, 1]), (3, rs_right.at[a, c, 0]),
                       (4, rs_left.at[a, c, 0]), (5, rs_right.at[a, c, 1])):
            arrived(ref, ys.at[1, a, c, n], yr.at[1, a, c, n])
        for e in range(2):
            part[a, c, y, e] = (part[a, c, y, e].astype(F32) + rs_left[a, c, e].astype(F32)
                                + rs_right[a, c, e].astype(F32)).astype(BF16)
        for o in range(1, NJ):
            jd = mate(o, 1)
            send(part.at[a, c, y, :, rows_of(jd), :], back.at[a, c, :, rows_of(j), :],
                 xs.at[1, a, c, o], xr.at[1, a, c, o], z * NJ + jd, y)
        own[1, a, c] = pltpu.make_async_copy(
            part.at[a, c, y, :, rows_of(j), :], back.at[a, c, :, rows_of(j), :], own_sem.at[1, a, c]
        )
        own[1, a, c].start()

    def combine(a, c):
        for o in range(1, NJ):
            js = mate(o, -1)
            arrived(back.at[a, c, :, rows_of(js), :], xs.at[1, a, c, o], xr.at[1, a, c, o])
        own[1, a, c].wait()
        got = back[a, c].reshape(EPL * ROWS, QW)
        chosen = pick[c]
        span = slice(ZHALF * c, ZHALF * (c + 1))
        if a == 0:
            dots = dot_nt(got, dense[span].reshape(ZHALF * TOK, QW))
            dots = jnp.where(chosen > 0, dots, 0.0).reshape(EPL, ROWS, ZHALF * TOK)
            dots = jnp.sum(dots, axis=1)
            for i in range(ZHALF):
                for e in range(2):
                    dsend[ZHALF * c + i, e] = dots[e * NJ : (e + 1) * NJ, i * TOK : (i + 1) * TOK]
            got = (got.astype(F32) * prow[c]).astype(BF16)
        zsend[a, span] = dot_tn(chosen, got).astype(BF16).reshape(ZHALF, TOK, QW)
        for i in range(ZHALF * c, ZHALF * (c + 1)):
            if i == 0:
                if a == 0:
                    dback[z] = dsend[0]
                continue
            zd = plane(i, 1)
            if a == 0:
                send(dsend.at[i], dback.at[z], zs.at[5, i], zr.at[5, i], zd * NJ + j, y)
            send(zsend.at[a, i], zback.at[a, i], zs.at[3 + a, i], zr.at[3 + a, i], zd * NJ + j, y)

    def finish(a, out):
        total = zsend[a, 0].astype(F32)
        for i in range(1, NZ):
            arrived(zback.at[a, i], zs.at[3 + a, i], zr.at[3 + a, i])
            total = total + zback[a, i].astype(F32)
        out[...] = total.astype(BF16)

    gather_send(1, 0)
    for i in (1, 2):
        gather_wait(1, i)
        gather_send(1, i)
    gather_send(0, 0)
    gather_wait(1, 3)
    gather_send(1, 3)
    routes(0)
    dispatch_cotangents(0)
    gather_wait(1, 4)
    gather_send(1, 4)
    for i in (1, 2):
        gather_wait(0, i)
        gather_send(0, i)
    for i in (5, 6):
        gather_wait(1, i)
        gather_send(1, i)
    ring_send(1, 0)
    gather_wait(1, 7)
    routes(1)
    dispatch_cotangents(1)
    for i in (3, 4):
        gather_wait(0, i)
        gather_send(0, i)
    dispatch_tokens(0)
    ring_forward(1, 0)
    ring_send(1, 1)
    for i in (5, 6):
        gather_wait(0, i)
        gather_send(0, i)
    gather_wait(0, 7)
    dispatch_tokens(1)
    ring_end(1, 0)
    for load in wloads:
        load.wait()
    ring_forward(1, 1)
    tokens_end(0)
    compute(0)
    scatter_send(0, 0)
    scatter_send(1, 0)
    ring_end(1, 1)
    scatter_add(0, 0)
    tokens_end(1)
    compute(1)
    scatter_send(0, 1)
    scatter_send(1, 1)
    scatter_add(1, 0)
    scatter_add(0, 1)
    scatter_add(1, 1)
    scatter_end(0, 0)

    def grads(e, carry):
        for q in range(NY):
            cols = slice(q * QW, (q + 1) * QW)
            for n, a, ref in ((0, 1, dwv), (1, 0, gwv), (2, 0, uwv)):
                ref[e, :, cols] = (dot_nn(acts[n, 0, e], rows[a, q, 0, e])
                                   + dot_nn(acts[n, 1, e], rows[a, q, 1, e])).astype(BF16)
        return carry

    lax.fori_loop(0, 2, grads, 0)
    stores = [pltpu.make_async_copy(a, b, loc.at[5 + n])
              for n, (a, b) in enumerate(((gwv, ggate), (uwv, gup), (dwv, gdown)))]
    for store in stores:
        store.start()

    combine(0, 0)
    scatter_end(0, 1)
    combine(0, 1)
    scatter_end(1, 0)
    combine(1, 0)
    scatter_end(1, 1)

    for i in range(1, NZ):
        zo = plane(i, -1)
        arrived(dback.at[zo], zs.at[5, i], zr.at[5, i])
    every = dback[...].reshape(TOK, TOK)
    eid = lax.div(eio, EPL) * EPL + lax.rem(eio, NJ) * 2 + lax.rem(lax.div(eio, NJ), 2)
    for k in range(TOP):
        hit = eid == ids[k : k + 1, :]
        dy[0, k : k + 1, :] = jnp.sum(jnp.where(hit, every, 0.0), axis=0, keepdims=True)
    for n, h in ((1, right), (2, opp), (3, left)):
        send(dy.at[0], dy.at[n], dys.at[n], dyr.at[n], ex, h)
    finish(0, layer_out)
    combine(1, 1)
    for n in range(1, NY):
        arrived(dy.at[n], dys.at[n], dyr.at[n])
    grad_probs = dy[0] + dy[1] + dy[2] + dy[3]
    grad_log[...] = probs * (grad_probs - jnp.sum(probs * grad_probs, axis=0, keepdims=True))
    finish(1, grad_tok)

    for store in stores:
        store.wait()
    for copy in sent:
        copy.wait_send()


def deliver_kernel(*refs):
    n = len(refs) // 2
    sems = refs[-1]
    copies = [pltpu.make_async_copy(refs[i], refs[n + i], sems.at[i]) for i in range(n)]
    for copy in copies:
        copy.start()
    for copy in copies:
        copy.wait()


def deliver(*arrays):
    spec = [pl.BlockSpec(memory_space=pl.ANY)] * len(arrays)
    return pl.pallas_call(
        deliver_kernel,
        out_shape=tuple(jax.ShapeDtypeStruct(a.shape, a.dtype) for a in arrays),
        in_specs=spec,
        out_specs=tuple(spec),
        scratch_shapes=[pltpu.SemaphoreType.DMA((len(arrays),))],
    )(*arrays)


def body(tokens, logits, expert_ids, gate_weight, up_weight, down_weight, grad_out):
    any_spec = pl.BlockSpec(memory_space=pl.ANY)
    vmem = pl.BlockSpec(memory_space=pltpu.VMEM)
    half = ZHALF * CAP * NJ
    weight = jax.ShapeDtypeStruct(gate_weight.shape, BF16)
    quarter = jax.ShapeDtypeStruct((TOK, QW), BF16)
    layer_out, grad_tok, grad_log, ggate, gup, gdown = pl.pallas_call(
        kernel,
        out_shape=(quarter, quarter, jax.ShapeDtypeStruct((TOP, TOK), F32), weight, weight, weight),
        in_specs=[any_spec, vmem, vmem, any_spec, any_spec, any_spec, any_spec],
        out_specs=(vmem, vmem, vmem, any_spec, any_spec, any_spec),
        scratch_shapes=[
            pltpu.VMEM((NZ, TOK, QW), BF16),
            pltpu.VMEM((NZ, TOK, NY * QW), BF16),
            pltpu.VMEM((2, TOK, TOK), F32),
            pltpu.VMEM((NZ, 2, EPL, TOK), F32),
            pltpu.VMEM((2, EPL * ROWS, ZHALF * TOK), BF16),
            pltpu.VMEM((2, EPL * ROWS, 1), F32),
            pltpu.VMEM((2, 2, half, QW), BF16),
            pltpu.VMEM((2, NY, 2, 2, half, QW), BF16),
            pltpu.VMEM(gate_weight.shape, BF16),
            pltpu.VMEM(gate_weight.shape, BF16),
            pltpu.VMEM(gate_weight.shape, BF16),
            pltpu.VMEM((3, 2, 2, gate_weight.shape[1], half), BF16),
            pltpu.VMEM((2, 2, NY, 2, half, QW), BF16),
            pltpu.VMEM((2, 2, 2, half, QW), BF16),
            pltpu.VMEM((2, 2, 2, half, QW), BF16),
            pltpu.VMEM((2, 2, 2, half, QW), BF16),
            pltpu.VMEM((2, 2, 2, half, QW), BF16),
            pltpu.VMEM((2, NZ, TOK, QW), BF16),
            pltpu.VMEM((2, NZ, TOK, QW), BF16),
            pltpu.VMEM((NZ, 2, NJ, TOK), F32),
            pltpu.VMEM((NZ, 2, NJ, TOK), F32),
            pltpu.VMEM((NY, TOP, TOK), F32),
            pltpu.SemaphoreType.DMA((6, NZ + 1)),
            pltpu.SemaphoreType.DMA((6, NZ + 1)),
            pltpu.SemaphoreType.DMA((2, 2, 2, NJ)),
            pltpu.SemaphoreType.DMA((2, 2, 2, NJ)),
            pltpu.SemaphoreType.DMA((2, 2, 2, 6)),
            pltpu.SemaphoreType.DMA((2, 2, 2, 6)),
            pltpu.SemaphoreType.DMA((NY,)),
            pltpu.SemaphoreType.DMA((NY,)),
            pltpu.SemaphoreType.DMA((8,)),
            pltpu.SemaphoreType.DMA((2, 2, 2)),
        ],
        compiler_params=pltpu.CompilerParams(
            collective_id=0, has_side_effects=True, vmem_limit_bytes=63 * 1024 * 1024
        ),
    )(tokens, expert_ids.T, logits.T, gate_weight, up_weight, down_weight, grad_out)
    layer_out, grad_tok, grad_log, ggate, gup, gdown = deliver(layer_out, grad_tok, grad_log, ggate, gup, gdown)
    return (layer_out, grad_tok, grad_log.T, ggate, gup, gdown)


def solution(mesh):
    placed = (
        P("expert", None),
        P("expert", None),
        P("expert", None),
        P("expert", "hid", None),
        P("expert", "hid", None),
        P("expert", "hid", None),
        P("expert", "hid"),
    )
    return jax.shard_map(
        body,
        mesh=mesh,
        in_specs=placed,
        out_specs=(
            P("expert", "hid"),
            P("expert", "hid"),
            P("expert", None),
            P("expert", "hid", None),
            P("expert", "hid", None),
            P("expert", "hid", None),
        ),
        check_vma=False,
    )
```

```python
import jax
import jax.numpy as jnp
from jax import lax
from jax.experimental import pallas as pl
from jax.experimental.pallas import tpu as pltpu
from jax.sharding import PartitionSpec as P

MESH = pl.DeviceIdType.MESH
F32, BF16 = jnp.float32, jnp.bfloat16
NZ, NJ, NY = 8, 8, 4
TOK, TOP, CAP, QW = 128, 8, 12, 512
ZHALF = 4
ROWS = ZHALF * CAP
EPL = 16
ORDER = (0, 1, -1, 2, -2, 3, -3, 4)


UNITS = (
    (0, 0, slice(0, 512)),
    (0, 1, slice(0, 512)),
    (1, 1, slice(0, 512)),
    (1, 0, slice(0, 256)),
    (1, 0, slice(256, 512)),
)


def dot_nt(a, b):
    return lax.dot_general(a, b, (((1,), (1,)), ((), ())), preferred_element_type=F32)


def dot_nn(a, b):
    return lax.dot_general(a, b, (((1,), (0,)), ((), ())), preferred_element_type=F32)


def dot_tn(a, b):
    return lax.dot_general(a, b, (((0,), (0,)), ((), ())), preferred_element_type=F32)


def kernel(
    tok, ids, logits, gw, uw, dw, go,
    layer_out, grad_tok, grad_log, ggate, gup, gdown,
    dense, densex, ep, info, pick, prow, slots, rows, gwv, uwv, dwv, acts, grad_act, part, rs_half, rs_left, rs_right,
    back, zsend, zback, dsend, dback, dy,
    zs, zr, xs, xr, ys, yr, rs, rr, bs, br, ts, tr, dys, dyr, loc, own_sem,
):
    ex = lax.axis_index("expert")
    y = lax.axis_index("hid")
    z, j = lax.div(ex, NJ), lax.rem(ex, NJ)
    right, left, opp = lax.rem(y + 1, NY), lax.rem(y + 3, NY), lax.rem(y + 2, NY)

    def plane(i, sign):
        return lax.rem(z + sign * ORDER[i] + NZ, NZ)

    def mate(o, sign):
        return lax.rem(j + sign * o + NJ, NJ)

    loads = [
        pltpu.make_async_copy(go, dense.at[0], loc.at[1]),
        pltpu.make_async_copy(tok.at[:, : 2 * QW], densex.at[0, 0], loc.at[0]),
        pltpu.make_async_copy(tok.at[:, 2 * QW :], densex.at[1, 0], loc.at[8]),
    ]
    wloads = [pltpu.make_async_copy(a, b, loc.at[2 + n]) for n, (a, b) in enumerate(((gw, gwv), (uw, uwv), (dw, dwv)))]
    for load in loads + wloads:
        load.start()

    barrier = pltpu.get_barrier_semaphore()
    for i in range(1, NZ):
        pl.semaphore_signal(barrier, inc=1, device_id=(plane(i, 1) * NJ + j, y), device_id_type=MESH)
    for o in range(1, NJ):
        pl.semaphore_signal(barrier, inc=1, device_id=(z * NJ + mate(o, 1), y), device_id_type=MESH)
    for h in (right, left, opp):
        pl.semaphore_signal(barrier, inc=1, device_id=(ex, h), device_id_type=MESH)

    exps = jnp.exp(logits[...])
    probs = exps / jnp.sum(exps, axis=0, keepdims=True)
    eio = lax.broadcasted_iota(jnp.int32, (TOK, TOK), 0)
    tio = lax.broadcasted_iota(jnp.int32, (TOK, TOK), 1)
    named = jnp.zeros((TOK, TOK), F32)
    weight = jnp.zeros((TOK, TOK), F32)
    for k in range(TOP):
        hit = eio == ids[k : k + 1, :]
        named = jnp.where(hit, 1.0, named)
        weight = jnp.where(hit, probs[k : k + 1, :], weight)
    earlier = dot_nn(named.astype(BF16), jnp.where(eio < tio, 1.0, 0.0).astype(BF16))
    ep[0] = jnp.where(named > 0.0, earlier, -1.0)
    ep[1] = weight
    info[0] = ep[:, pl.ds(pl.multiple_of(z * EPL, EPL), EPL), :]

    for load in loads:
        load.wait()
    pl.semaphore_wait(barrier, NZ + NJ + NY - 3)

    sent = []

    def send(src, dst, ssem, rsem, e, h):
        copy = pltpu.make_async_remote_copy(
            src_ref=src, dst_ref=dst, send_sem=ssem, recv_sem=rsem, device_id=(e, h), device_id_type=MESH
        )
        copy.start()
        sent.append(copy)

    def arrived(ref, ssem, rsem):
        pltpu.make_async_remote_copy(
            src_ref=ref, dst_ref=ref, send_sem=ssem, recv_sem=rsem, device_id=(ex, right), device_id_type=MESH
        ).wait_recv()

    def gather_piece(a, i, half):
        ref = dense.at[i] if a == 2 else densex.at[a, i]
        return ref if half is None else ref.at[half * (TOK // 2) : (half + 1) * (TOK // 2)]

    def gather_send(a, i):
        for n in (1, 2) if i == 0 else (i + 2,):
            down = n % 2 == 1 if i == 0 else i % 2 == 1
            half = None
            if n > 6:
                half, n = n - 7, 7
            sem = n if half is None else NZ - 1 + half
            send(gather_piece(a, i, half), gather_piece(a, n, half), zs.at[a, sem], zr.at[a, sem],
                 plane(1, -1 if down else 1) * NJ + j, y)

    def gather_wait(a, i):
        if i < NZ - 1:
            arrived(gather_piece(a, i, None), zs.at[a, i], zr.at[a, i])
        else:
            for half in range(2):
                arrived(gather_piece(a, i, half), zs.at[a, i + half], zr.at[a, i + half])

    def gather_pass(a, *blocks):
        for i in blocks:
            gather_wait(a, i)
            gather_send(a, i)

    for i in range(1, NZ):
        zd = plane(i, -1)
        send(ep.at[:, pl.ds(pl.multiple_of(zd * EPL, EPL), EPL), :], info.at[i],
             zs.at[3, i], zr.at[3, i], zd * NJ + j, y)

    rio = lax.broadcasted_iota(jnp.int32, (ROWS, ZHALF * TOK), 0).astype(F32)

    def routes(c):
        span = range(ZHALF * c, ZHALF * (c + 1))
        for i in span:
            if i > 0:
                arrived(info.at[i], zs.at[3, i], zr.at[3, i])
        place = jnp.concatenate(
            [jnp.where(info[i, 0] >= 0.0, info[i, 0] + float(CAP * (i % ZHALF)), -1.0) for i in span], axis=1
        )
        share = jnp.concatenate([info[i, 1] for i in span], axis=1)
        for e in range(EPL):
            first = (e % 2) * NJ * ROWS + (e // 2) * ROWS
            mask = rio == place[e : e + 1, :]
            pick[c, first : first + ROWS, :] = jnp.where(mask, 1.0, 0.0).astype(BF16)
            prow[c, first : first + ROWS, :] = jnp.sum(
                jnp.where(mask, share[e : e + 1, :], 0.0), axis=1, keepdims=True
            )

    own = {}

    def rows_of(d):
        return pl.ds(pl.multiple_of(d * ROWS, ROWS), ROWS)

    staged = {0: [], 1: []}

    def dispatch_tokens(h, c):
        span = slice(ZHALF * c, ZHALF * (c + 1))
        pair = slice(2 * h, 2 * h + 2)
        for q in range(2):
            block = densex[h, span, :, q * QW : (q + 1) * QW].reshape(ZHALF * TOK, QW)
            part[1, c, 2 * h + q] = dot_nn(pick[c], block).astype(BF16).reshape(2, NJ * ROWS, QW)
        before = len(sent)
        for o in range(1, NJ):
            jd = mate(o, 1)
            send(part.at[1, c, pair, :, rows_of(jd), :], rows.at[0, pair, c, :, rows_of(j), :],
                 xs.at[h, c, o], xr.at[h, c, o], z * NJ + jd, y)
        staged[c] += sent[before:]
        del sent[before:]
        own[h, c] = pltpu.make_async_copy(
            part.at[1, c, pair, :, rows_of(j), :], rows.at[0, pair, c, :, rows_of(j), :], own_sem.at[h, c]
        )
        own[h, c].start()

    def tokens_half(h, c):
        for o in range(1, NJ):
            js = mate(o, -1)
            arrived(rows.at[0, 2 * h : 2 * h + 2, c, :, rows_of(js), :], xs.at[h, c, o], xr.at[h, c, o])
        own[h, c].wait()

    def tokens_end(c):
        for copy in staged[c]:
            copy.wait_send()

    def dispatch_cotangents(c):
        block = dense[ZHALF * c : ZHALF * (c + 1)].reshape(ZHALF * TOK, QW)
        for e in range(2):
            some = slice(e * NJ * ROWS, (e + 1) * NJ * ROWS)
            slots[c, e] = (dot_nn(pick[c, some], block) * prow[c, some]).astype(BF16)
            for o in range(1, NJ):
                jd = mate(o, 1)
                send(slots.at[c, e, rows_of(jd), :], rows.at[1, y, c, e, rows_of(j), :],
                     xs.at[2 + e, c, o], xr.at[2 + e, c, o], z * NJ + jd, y)
            own[2 + e, c] = pltpu.make_async_copy(
                slots.at[c, e, rows_of(j), :], rows.at[1, y, c, e, rows_of(j), :], own_sem.at[2 + e, c]
            )
            own[2 + e, c].start()

    def ring_send(a, c):
        for e in range(2):
            for o in range(1, NJ):
                js = mate(o, -1)
                arrived(rows.at[a, y, c, e, rows_of(js), :], xs.at[2 + e, c, o], xr.at[2 + e, c, o])
            own[2 + e, c].wait()
            piece = rows.at[a, y, c, e]
            send(piece, piece, ys.at[c, e], yr.at[c, e], ex, right)
            send(piece, piece, ys.at[c, 2 + e], yr.at[c, 2 + e], ex, left)

    def ring_forward(a, c):
        arrived(rows.at[a, left, c, 0], ys.at[c, 0], yr.at[c, 0])
        piece = rows.at[a, left, c, 0]
        send(piece, piece, ys.at[c, 4], yr.at[c, 4], ex, right)
        arrived(rows.at[a, right, c, 1], ys.at[c, 3], yr.at[c, 3])
        piece = rows.at[a, right, c, 1]
        send(piece, piece, ys.at[c, 5], yr.at[c, 5], ex, left)

    def ring_end(a, c):
        for n, (src, e) in enumerate(((left, 0), (left, 1), (right, 0), (right, 1), (opp, 0), (opp, 1))):
            if n not in (0, 3):
                arrived(rows.at[a, src, c, e], ys.at[c, n], yr.at[c, n])

    def compute_out(c):
        def expert(e, carry):
            pre_gate = pre_up = grad_hidden = 0.0
            for q in range(NY):
                cols = slice(q * QW, (q + 1) * QW)
                x = rows[0, q, c, e]
                pre_gate += dot_nt(x, gwv[e, :, cols])
                pre_up += dot_nt(x, uwv[e, :, cols])
                grad_hidden += dot_nt(rows[1, q, c, e], dwv[e, :, cols])
            sig = jax.nn.sigmoid(pre_gate)
            act = pre_gate * sig
            hidden = act * pre_up
            gpg = grad_hidden * pre_up * sig * (1.0 + pre_gate * (1.0 - sig))
            gpu = grad_hidden * act
            acts[0, c, e] = hidden.T.astype(BF16)
            acts[1, c, e] = gpg.T.astype(BF16)
            acts[2, c, e] = gpu.T.astype(BF16)
            grad_act[0, e] = gpg.astype(BF16)
            grad_act[1, e] = gpu.astype(BF16)
            hidden = hidden.astype(BF16)
            for q in range(NY):
                part[0, c, q, e] = dot_nn(hidden, dwv[e, :, q * QW : (q + 1) * QW]).astype(BF16)
            return carry

        lax.fori_loop(0, 2, expert, 0)

    def compute_dx(c):
        def expert(e, carry):
            for q in range(NY):
                cols = slice(q * QW, (q + 1) * QW)
                part[1, c, q, e] = (
                    dot_nn(grad_act[0, e], gwv[e, :, cols]) + dot_nn(grad_act[1, e], uwv[e, :, cols])
                ).astype(BF16)
            return carry

        lax.fori_loop(0, 2, expert, 0)

    def scatter_first(u):
        a, c, f = UNITS[u]
        for dst, e, target, n, h in ((opp, 0, rs_half, 0, right), (opp, 1, rs_half, 1, left)):
            send(part.at[a, c, dst, e, :, f], target.at[a, c, e, :, f], rs.at[u, n], rr.at[u, n], ex, h)

    def scatter_plain(u):
        a, c, f = UNITS[u]
        for dst, e, target, n, h in ((right, 1, rs_left, 2, right), (left, 0, rs_right, 3, left)):
            send(part.at[a, c, dst, e, :, f], target.at[a, c, e, :, f], rs.at[u, n], rr.at[u, n], ex, h)

    def scatter_add(u):
        a, c, f = UNITS[u]
        for dst, e, target, h in ((right, 0, rs_left, right), (left, 1, rs_right, left)):
            arrived(rs_half.at[a, c, e, :, f], rs.at[u, e], rr.at[u, e])
            part[a, c, dst, e, :, f] = (
                part[a, c, dst, e, :, f].astype(F32) + rs_half[a, c, e, :, f].astype(F32)
            ).astype(BF16)
            send(part.at[a, c, dst, e, :, f], target.at[a, c, e, :, f], rs.at[u, 4 + e], rr.at[u, 4 + e], ex, h)

    def scatter_end(u):
        a, c, f = UNITS[u]
        for n, e, ref in ((2, 1, rs_left), (3, 0, rs_right), (4, 0, rs_left), (5, 1, rs_right)):
            arrived(ref.at[a, c, e, :, f], rs.at[u, n], rr.at[u, n])
        for e in range(2):
            part[a, c, y, e, :, f] = (
                part[a, c, y, e, :, f].astype(F32)
                + rs_left[a, c, e, :, f].astype(F32)
                + rs_right[a, c, e, :, f].astype(F32)
            ).astype(BF16)
        for o in range(1, NJ):
            jd = mate(o, 1)
            send(part.at[a, c, y, :, rows_of(jd), f], back.at[a, c, :, rows_of(j), f],
                 bs.at[u, o], br.at[u, o], z * NJ + jd, y)
        own[u] = pltpu.make_async_copy(
            part.at[a, c, y, :, rows_of(j), f], back.at[a, c, :, rows_of(j), f], bs.at[u, 0]
        )
        own[u].start()

    def combine(u):
        a, c, f = UNITS[u]
        for o in range(1, NJ):
            js = mate(o, -1)
            arrived(back.at[a, c, :, rows_of(js), f], bs.at[u, o], br.at[u, o])
        own[u].wait()
        width = f.stop - f.start
        got = back[a, c, :, :, f].reshape(EPL * ROWS, width)
        chosen = pick[c]
        span = slice(ZHALF * c, ZHALF * (c + 1))
        if a == 0:
            dots = dot_nt(got, dense[span].reshape(ZHALF * TOK, QW))
            dots = jnp.where(chosen > 0, dots, 0.0).reshape(EPL, ROWS, ZHALF * TOK)
            dots = jnp.sum(dots, axis=1)
            for i in range(ZHALF):
                for e in range(2):
                    dsend[ZHALF * c + i, e] = dots[e * NJ : (e + 1) * NJ, i * TOK : (i + 1) * TOK]
            got = (got.astype(F32) * prow[c]).astype(BF16)
        zsend[a, span, :, f] = dot_tn(chosen, got).astype(BF16).reshape(ZHALF, TOK, width)
        for i in range(ZHALF * c, ZHALF * (c + 1)):
            if i == 0:
                if a == 0:
                    dback[z] = dsend[0]
                continue
            zd = plane(i, 1)
            if a == 0:
                send(dsend.at[i], dback.at[z], zs.at[4, i], zr.at[4, i], zd * NJ + j, y)
            send(zsend.at[a, i, :, f], zback.at[a, i, :, f], ts.at[u, i], tr.at[u, i], zd * NJ + j, y)

    def finish(a, out):
        for u, (b, c, f) in enumerate(UNITS):
            if a == b:
                for i in range(max(1, ZHALF * c), ZHALF * (c + 1)):
                    arrived(zback.at[a, i, :, f], ts.at[u, i], tr.at[u, i])
        total = zsend[a, 0].astype(F32)
        for i in range(1, NZ):
            total = total + zback[a, i].astype(F32)
        out[...] = total.astype(BF16)

    def grads(e, carry):
        for q in range(NY):
            cols = slice(q * QW, (q + 1) * QW)
            for n, a, ref in ((0, 1, dwv), (1, 0, gwv), (2, 0, uwv)):
                ref[e, :, cols] = (dot_nn(acts[n, 0, e], rows[a, q, 0, e])
                                   + dot_nn(acts[n, 1, e], rows[a, q, 1, e])).astype(BF16)
        return carry

    gather_send(2, 0)
    gather_pass(2, 1, 2)
    gather_send(0, 0)
    routes(0)
    gather_pass(2, 3, 4)
    dispatch_cotangents(0)
    gather_pass(0, 1, 2)
    gather_send(1, 0)
    gather_pass(2, 5, 6)
    routes(1)
    gather_wait(0, 3)
    dispatch_tokens(0, 0)
    ring_send(1, 0)
    gather_wait(2, 7)
    dispatch_cotangents(1)
    gather_pass(1, 1, 2)
    gather_send(0, 3)
    gather_pass(0, 4)
    gather_wait(1, 3)
    dispatch_tokens(1, 0)
    gather_send(1, 3)
    gather_pass(1, 4)
    ring_forward(1, 0)
    ring_send(1, 1)
    gather_pass(0, 5, 6)
    gather_wait(0, 7)
    tokens_half(0, 0)
    dispatch_tokens(0, 1)
    gather_pass(1, 5, 6)
    gather_wait(1, 7)
    ring_end(1, 0)
    for load in wloads:
        load.wait()
    tokens_half(1, 0)
    dispatch_tokens(1, 1)
    ring_forward(1, 1)
    tokens_end(0)
    compute_out(0)
    scatter_first(0)
    scatter_plain(0)
    compute_dx(0)
    ring_end(1, 1)
    scatter_add(0)
    tokens_half(0, 1)
    tokens_half(1, 1)
    tokens_end(1)
    compute_out(1)
    scatter_first(1)
    scatter_plain(1)
    compute_dx(1)
    scatter_first(2)
    scatter_end(0)
    scatter_add(1)
    combine(0)
    scatter_plain(2)
    scatter_add(2)
    scatter_first(3)
    lax.fori_loop(0, 2, grads, 0)
    stores = [pltpu.make_async_copy(a, b, loc.at[5 + n])
              for n, (a, b) in enumerate(((gwv, ggate), (uwv, gup), (dwv, gdown)))]
    for store in stores:
        store.start()

    scatter_end(1)
    scatter_plain(3)
    scatter_add(3)
    scatter_first(4)
    scatter_plain(4)
    combine(1)
    scatter_end(2)
    scatter_add(4)
    combine(2)
    scatter_end(3)
    combine(3)
    scatter_end(4)

    for i in range(1, NZ):
        zo = plane(i, -1)
        arrived(dback.at[zo], zs.at[4, i], zr.at[4, i])
    every = dback[...].reshape(TOK, TOK)
    eid = lax.div(eio, EPL) * EPL + lax.rem(eio, NJ) * 2 + lax.rem(lax.div(eio, NJ), 2)
    for k in range(TOP):
        hit = eid == ids[k : k + 1, :]
        dy[0, k : k + 1, :] = jnp.sum(jnp.where(hit, every, 0.0), axis=0, keepdims=True)
    for n, h in ((1, right), (2, opp), (3, left)):
        send(dy.at[0], dy.at[n], dys.at[n], dyr.at[n], ex, h)
    finish(0, layer_out)
    combine(4)
    for n in range(1, NY):
        arrived(dy.at[n], dys.at[n], dyr.at[n])
    grad_probs = dy[0] + dy[1] + dy[2] + dy[3]
    grad_log[...] = probs * (grad_probs - jnp.sum(probs * grad_probs, axis=0, keepdims=True))
    finish(1, grad_tok)

    for store in stores:
        store.wait()
    for copy in sent:
        copy.wait_send()


def deliver_kernel(*refs):
    n = (len(refs) - 2) // 3
    src, dst, held = refs[:n], refs[n : 2 * n], refs[2 * n : 3 * n]
    ins = [pltpu.make_async_copy(src[i], held[i], refs[-2].at[i]) for i in range(n)]
    outs = [pltpu.make_async_copy(held[i], dst[i], refs[-1].at[i]) for i in range(n)]
    for copy in ins:
        copy.start()
    for copy_in, copy_out in zip(ins, outs):
        copy_in.wait()
        copy_out.start()
    for copy in outs:
        copy.wait()


def deliver(*arrays):
    n = len(arrays)
    spec = [pl.BlockSpec(memory_space=pl.ANY)] * n
    return pl.pallas_call(
        deliver_kernel,
        out_shape=tuple(jax.ShapeDtypeStruct(a.shape, a.dtype) for a in arrays),
        in_specs=spec,
        out_specs=tuple(spec),
        scratch_shapes=[pltpu.VMEM(a.shape, a.dtype) for a in arrays]
        + [pltpu.SemaphoreType.DMA((n,)), pltpu.SemaphoreType.DMA((n,))],
        compiler_params=pltpu.CompilerParams(vmem_limit_bytes=62 * 1024 * 1024),
    )(*arrays)


def body(tokens, logits, expert_ids, gate_weight, up_weight, down_weight, grad_out):
    any_spec = pl.BlockSpec(memory_space=pl.ANY)
    vmem = pl.BlockSpec(memory_space=pltpu.VMEM)
    half = ZHALF * CAP * NJ
    weight = jax.ShapeDtypeStruct(gate_weight.shape, BF16)
    quarter = jax.ShapeDtypeStruct((TOK, QW), BF16)
    layer_out, grad_tok, grad_log, ggate, gup, gdown = pl.pallas_call(
        kernel,
        out_shape=(quarter, quarter, jax.ShapeDtypeStruct((TOP, TOK), F32), weight, weight, weight),
        in_specs=[any_spec, vmem, vmem, any_spec, any_spec, any_spec, any_spec],
        out_specs=(vmem, vmem, vmem, any_spec, any_spec, any_spec),
        scratch_shapes=[
            pltpu.VMEM((NZ, TOK, QW), BF16),
            pltpu.VMEM((2, NZ, TOK, 2 * QW), BF16),
            pltpu.VMEM((2, TOK, TOK), F32),
            pltpu.VMEM((NZ, 2, EPL, TOK), F32),
            pltpu.VMEM((2, EPL * ROWS, ZHALF * TOK), BF16),
            pltpu.VMEM((2, EPL * ROWS, 1), F32),
            pltpu.VMEM((2, 2, half, QW), BF16),
            pltpu.VMEM((2, NY, 2, 2, half, QW), BF16),
            pltpu.VMEM(gate_weight.shape, BF16),
            pltpu.VMEM(gate_weight.shape, BF16),
            pltpu.VMEM(gate_weight.shape, BF16),
            pltpu.VMEM((3, 2, 2, gate_weight.shape[1], half), BF16),
            pltpu.VMEM((2, 2, half, gate_weight.shape[1]), BF16),
            pltpu.VMEM((2, 2, NY, 2, half, QW), BF16),
            pltpu.VMEM((2, 2, 2, half, QW), BF16),
            pltpu.VMEM((2, 2, 2, half, QW), BF16),
            pltpu.VMEM((2, 2, 2, half, QW), BF16),
            pltpu.VMEM((2, 2, 2, half, QW), BF16),
            pltpu.VMEM((2, NZ, TOK, QW), BF16),
            pltpu.VMEM((2, NZ, TOK, QW), BF16),
            pltpu.VMEM((NZ, 2, NJ, TOK), F32),
            pltpu.VMEM((NZ, 2, NJ, TOK), F32),
            pltpu.VMEM((NY, TOP, TOK), F32),
            pltpu.SemaphoreType.DMA((5, NZ + 1)),
            pltpu.SemaphoreType.DMA((5, NZ + 1)),
            pltpu.SemaphoreType.DMA((4, 2, NJ)),
            pltpu.SemaphoreType.DMA((4, 2, NJ)),
            pltpu.SemaphoreType.DMA((2, 6)),
            pltpu.SemaphoreType.DMA((2, 6)),
            pltpu.SemaphoreType.DMA((len(UNITS), 6)),
            pltpu.SemaphoreType.DMA((len(UNITS), 6)),
            pltpu.SemaphoreType.DMA((len(UNITS), NJ)),
            pltpu.SemaphoreType.DMA((len(UNITS), NJ)),
            pltpu.SemaphoreType.DMA((len(UNITS), NZ)),
            pltpu.SemaphoreType.DMA((len(UNITS), NZ)),
            pltpu.SemaphoreType.DMA((NY,)),
            pltpu.SemaphoreType.DMA((NY,)),
            pltpu.SemaphoreType.DMA((9,)),
            pltpu.SemaphoreType.DMA((4, 2)),
        ],
        compiler_params=pltpu.CompilerParams(
            collective_id=0, has_side_effects=True, vmem_limit_bytes=63 * 1024 * 1024
        ),
    )(tokens, expert_ids.T, logits.T, gate_weight, up_weight, down_weight, grad_out)
    layer_out, grad_tok, grad_log, ggate, gup, gdown = deliver(layer_out, grad_tok, grad_log, ggate, gup, gdown)
    return (layer_out, grad_tok, grad_log.T, ggate, gup, gdown)


def solution(mesh):
    placed = (
        P("expert", None),
        P("expert", None),
        P("expert", None),
        P("expert", "hid", None),
        P("expert", "hid", None),
        P("expert", "hid", None),
        P("expert", "hid"),
    )
    return jax.shard_map(
        body,
        mesh=mesh,
        in_specs=placed,
        out_specs=(
            P("expert", "hid"),
            P("expert", "hid"),
            P("expert", None),
            P("expert", "hid", None),
            P("expert", "hid", None),
            P("expert", "hid", None),
        ),
        check_vma=False,
    )
```

```python
import jax
import jax.numpy as jnp
from jax import lax
from jax.experimental import pallas as pl
from jax.experimental.pallas import tpu as pltpu
from jax.sharding import PartitionSpec as P

MESH = pl.DeviceIdType.MESH
F32, BF16 = jnp.float32, jnp.bfloat16
NZ, NJ, NY = 8, 8, 4
TOK, TOP, CAP, QW = 128, 8, 12, 512
ZHALF = 4
ROWS = ZHALF * CAP
EPL = 16
ORDER = (0, 1, -1, 2, -2, 3, -3, 4)


UNITS = (
    (0, 0, slice(0, 512)),
    (0, 1, slice(0, 512)),
    (1, 1, slice(0, 512)),
    (1, 0, slice(0, 256)),
    (1, 0, slice(256, 512)),
)


def dot_nt(a, b):
    return lax.dot_general(a, b, (((1,), (1,)), ((), ())), preferred_element_type=F32)


def dot_nn(a, b):
    return lax.dot_general(a, b, (((1,), (0,)), ((), ())), preferred_element_type=F32)


def dot_tn(a, b):
    return lax.dot_general(a, b, (((0,), (0,)), ((), ())), preferred_element_type=F32)


def kernel(
    tok, ids, logits, gw, uw, dw, go,
    layer_out, grad_tok, grad_log, ggate, gup, gdown,
    dense, densex, ep, info, pick, prow, slots, rows, gwv, uwv, dwv, acts, grad_act, part, rs_half, rs_left, rs_right,
    back, zsend, zback, dsend, dback, dy,
    zs, zr, xs, xr, ys, yr, rs, rr, bs, br, ts, tr, dys, dyr, loc, own_sem,
):
    ex = lax.axis_index("expert")
    y = lax.axis_index("hid")
    z, j = lax.div(ex, NJ), lax.rem(ex, NJ)
    right, left, opp = lax.rem(y + 1, NY), lax.rem(y + 3, NY), lax.rem(y + 2, NY)

    def plane(i, sign):
        return lax.rem(z + sign * ORDER[i] + NZ, NZ)

    def mate(o, sign):
        return lax.rem(j + sign * o + NJ, NJ)

    loads = [
        pltpu.make_async_copy(go, dense.at[0], loc.at[1]),
        pltpu.make_async_copy(tok.at[:, : 2 * QW], densex.at[0, 0], loc.at[0]),
        pltpu.make_async_copy(tok.at[:, 2 * QW :], densex.at[1, 0], loc.at[8]),
    ]
    wloads = [pltpu.make_async_copy(a, b, loc.at[2 + n]) for n, (a, b) in enumerate(((gw, gwv), (uw, uwv), (dw, dwv)))]
    for load in loads + wloads:
        load.start()

    barrier = pltpu.get_barrier_semaphore()
    for i in range(1, NZ):
        pl.semaphore_signal(barrier, inc=1, device_id=(plane(i, 1) * NJ + j, y), device_id_type=MESH)
    for o in range(1, NJ):
        pl.semaphore_signal(barrier, inc=1, device_id=(z * NJ + mate(o, 1), y), device_id_type=MESH)
    for h in (right, left, opp):
        pl.semaphore_signal(barrier, inc=1, device_id=(ex, h), device_id_type=MESH)

    exps = jnp.exp(logits[...])
    probs = exps / jnp.sum(exps, axis=0, keepdims=True)
    eio = lax.broadcasted_iota(jnp.int32, (TOK, TOK), 0)
    tio = lax.broadcasted_iota(jnp.int32, (TOK, TOK), 1)
    named = jnp.zeros((TOK, TOK), F32)
    weight = jnp.zeros((TOK, TOK), F32)
    for k in range(TOP):
        hit = eio == ids[k : k + 1, :]
        named = jnp.where(hit, 1.0, named)
        weight = jnp.where(hit, probs[k : k + 1, :], weight)
    earlier = dot_nn(named.astype(BF16), jnp.where(eio < tio, 1.0, 0.0).astype(BF16))
    ep[0] = jnp.where(named > 0.0, earlier, -1.0)
    ep[1] = weight
    info[0] = ep[:, pl.ds(pl.multiple_of(z * EPL, EPL), EPL), :]

    for load in loads:
        load.wait()
    pl.semaphore_wait(barrier, NZ + NJ + NY - 3)

    sent = []

    def send(src, dst, ssem, rsem, e, h):
        copy = pltpu.make_async_remote_copy(
            src_ref=src, dst_ref=dst, send_sem=ssem, recv_sem=rsem, device_id=(e, h), device_id_type=MESH
        )
        copy.start()
        sent.append(copy)

    def arrived(ref, ssem, rsem):
        pltpu.make_async_remote_copy(
            src_ref=ref, dst_ref=ref, send_sem=ssem, recv_sem=rsem, device_id=(ex, right), device_id_type=MESH
        ).wait_recv()

    def gather_piece(a, i, half):
        ref = dense.at[i] if a == 2 else densex.at[a, i]
        return ref if half is None else ref.at[half * (TOK // 2) : (half + 1) * (TOK // 2)]

    def gather_send(a, i):
        for n in (1, 2) if i == 0 else (i + 2,):
            down = n % 2 == 1 if i == 0 else i % 2 == 1
            half = None
            if n > 6:
                half, n = n - 7, 7
            sem = n if half is None else NZ - 1 + half
            send(gather_piece(a, i, half), gather_piece(a, n, half), zs.at[a, sem], zr.at[a, sem],
                 plane(1, -1 if down else 1) * NJ + j, y)

    def gather_wait(a, i):
        if i < NZ - 1:
            arrived(gather_piece(a, i, None), zs.at[a, i], zr.at[a, i])
        else:
            for half in range(2):
                arrived(gather_piece(a, i, half), zs.at[a, i + half], zr.at[a, i + half])

    def gather_pass(a, *blocks):
        for i in blocks:
            gather_wait(a, i)
            gather_send(a, i)

    for i in range(1, NZ):
        zd = plane(i, -1)
        send(ep.at[:, pl.ds(pl.multiple_of(zd * EPL, EPL), EPL), :], info.at[i],
             zs.at[3, i], zr.at[3, i], zd * NJ + j, y)

    rio = lax.broadcasted_iota(jnp.int32, (ROWS, ZHALF * TOK), 0).astype(F32)

    def routes(c):
        span = range(ZHALF * c, ZHALF * (c + 1))
        for i in span:
            if i > 0:
                arrived(info.at[i], zs.at[3, i], zr.at[3, i])
        place = jnp.concatenate(
            [jnp.where(info[i, 0] >= 0.0, info[i, 0] + float(CAP * (i % ZHALF)), -1.0) for i in span], axis=1
        )
        share = jnp.concatenate([info[i, 1] for i in span], axis=1)
        for e in range(EPL):
            first = (e % 2) * NJ * ROWS + (e // 2) * ROWS
            mask = rio == place[e : e + 1, :]
            pick[c, first : first + ROWS, :] = jnp.where(mask, 1.0, 0.0).astype(BF16)
            prow[c, first : first + ROWS, :] = jnp.sum(
                jnp.where(mask, share[e : e + 1, :], 0.0), axis=1, keepdims=True
            )

    own = {}

    def rows_of(d):
        return pl.ds(pl.multiple_of(d * ROWS, ROWS), ROWS)

    staged = {0: [], 1: []}

    def dispatch_tokens(h, c):
        span = slice(ZHALF * c, ZHALF * (c + 1))
        pair = slice(2 * h, 2 * h + 2)
        for q in range(2):
            block = densex[h, span, :, q * QW : (q + 1) * QW].reshape(ZHALF * TOK, QW)
            part[1, c, 2 * h + q] = dot_nn(pick[c], block).astype(BF16).reshape(2, NJ * ROWS, QW)
        before = len(sent)
        for o in range(1, NJ):
            jd = mate(o, 1)
            send(part.at[1, c, pair, :, rows_of(jd), :], rows.at[0, pair, c, :, rows_of(j), :],
                 xs.at[h, c, o], xr.at[h, c, o], z * NJ + jd, y)
        staged[c] += sent[before:]
        del sent[before:]
        own[h, c] = pltpu.make_async_copy(
            part.at[1, c, pair, :, rows_of(j), :], rows.at[0, pair, c, :, rows_of(j), :], own_sem.at[h, c]
        )
        own[h, c].start()

    def tokens_half(h, c):
        for o in range(1, NJ):
            js = mate(o, -1)
            arrived(rows.at[0, 2 * h : 2 * h + 2, c, :, rows_of(js), :], xs.at[h, c, o], xr.at[h, c, o])
        own[h, c].wait()

    def tokens_end(c):
        for copy in staged[c]:
            copy.wait_send()

    def dispatch_cotangents(c):
        block = dense[ZHALF * c : ZHALF * (c + 1)].reshape(ZHALF * TOK, QW)
        for e in range(2):
            some = slice(e * NJ * ROWS, (e + 1) * NJ * ROWS)
            slots[c, e] = (dot_nn(pick[c, some], block) * prow[c, some]).astype(BF16)
            for o in range(1, NJ):
                jd = mate(o, 1)
                send(slots.at[c, e, rows_of(jd), :], rows.at[1, y, c, e, rows_of(j), :],
                     xs.at[2 + e, c, o], xr.at[2 + e, c, o], z * NJ + jd, y)
            own[2 + e, c] = pltpu.make_async_copy(
                slots.at[c, e, rows_of(j), :], rows.at[1, y, c, e, rows_of(j), :], own_sem.at[2 + e, c]
            )
            own[2 + e, c].start()

    def ring_send(a, c):
        for e in range(2):
            for o in range(1, NJ):
                js = mate(o, -1)
                arrived(rows.at[a, y, c, e, rows_of(js), :], xs.at[2 + e, c, o], xr.at[2 + e, c, o])
            own[2 + e, c].wait()
            piece = rows.at[a, y, c, e]
            send(piece, piece, ys.at[c, e], yr.at[c, e], ex, right)
            send(piece, piece, ys.at[c, 2 + e], yr.at[c, 2 + e], ex, left)

    def ring_forward(a, c):
        arrived(rows.at[a, left, c, 0], ys.at[c, 0], yr.at[c, 0])
        piece = rows.at[a, left, c, 0]
        send(piece, piece, ys.at[c, 4], yr.at[c, 4], ex, right)
        arrived(rows.at[a, right, c, 1], ys.at[c, 3], yr.at[c, 3])
        piece = rows.at[a, right, c, 1]
        send(piece, piece, ys.at[c, 5], yr.at[c, 5], ex, left)

    def ring_end(a, c):
        for n, (src, e) in enumerate(((left, 0), (left, 1), (right, 0), (right, 1), (opp, 0), (opp, 1))):
            if n not in (0, 3):
                arrived(rows.at[a, src, c, e], ys.at[c, n], yr.at[c, n])

    def compute_out(c):
        def expert(e, carry):
            pre_gate = pre_up = grad_hidden = 0.0
            for q in range(NY):
                cols = slice(q * QW, (q + 1) * QW)
                x = rows[0, q, c, e]
                pre_gate += dot_nt(x, gwv[e, :, cols])
                pre_up += dot_nt(x, uwv[e, :, cols])
                grad_hidden += dot_nt(rows[1, q, c, e], dwv[e, :, cols])
            sig = jax.nn.sigmoid(pre_gate)
            act = pre_gate * sig
            hidden = act * pre_up
            gpg = grad_hidden * pre_up * sig * (1.0 + pre_gate * (1.0 - sig))
            gpu = grad_hidden * act
            acts[0, c, e] = hidden.T.astype(BF16)
            acts[1, c, e] = gpg.T.astype(BF16)
            acts[2, c, e] = gpu.T.astype(BF16)
            grad_act[0, e] = gpg.astype(BF16)
            grad_act[1, e] = gpu.astype(BF16)
            hidden = hidden.astype(BF16)
            for q in range(NY):
                part[0, c, q, e] = dot_nn(hidden, dwv[e, :, q * QW : (q + 1) * QW]).astype(BF16)
            return carry

        lax.fori_loop(0, 2, expert, 0)

    def compute_dx(c):
        def expert(e, carry):
            for q in range(NY):
                cols = slice(q * QW, (q + 1) * QW)
                part[1, c, q, e] = (
                    dot_nn(grad_act[0, e], gwv[e, :, cols]) + dot_nn(grad_act[1, e], uwv[e, :, cols])
                ).astype(BF16)
            return carry

        lax.fori_loop(0, 2, expert, 0)

    def scatter_first(u):
        a, c, f = UNITS[u]
        for dst, e, target, n, h in ((opp, 0, rs_half, 0, right), (opp, 1, rs_half, 1, left)):
            send(part.at[a, c, dst, e, :, f], target.at[a, c, e, :, f], rs.at[u, n], rr.at[u, n], ex, h)

    def scatter_plain(u):
        a, c, f = UNITS[u]
        for dst, e, target, n, h in ((right, 1, rs_left, 2, right), (left, 0, rs_right, 3, left)):
            send(part.at[a, c, dst, e, :, f], target.at[a, c, e, :, f], rs.at[u, n], rr.at[u, n], ex, h)

    def scatter_add(u):
        a, c, f = UNITS[u]
        for dst, e, target, h in ((right, 0, rs_left, right), (left, 1, rs_right, left)):
            arrived(rs_half.at[a, c, e, :, f], rs.at[u, e], rr.at[u, e])
            part[a, c, dst, e, :, f] = (
                part[a, c, dst, e, :, f].astype(F32) + rs_half[a, c, e, :, f].astype(F32)
            ).astype(BF16)
            send(part.at[a, c, dst, e, :, f], target.at[a, c, e, :, f], rs.at[u, 4 + e], rr.at[u, 4 + e], ex, h)

    def scatter_end(u):
        a, c, f = UNITS[u]
        for n, e, ref in ((2, 1, rs_left), (3, 0, rs_right), (4, 0, rs_left), (5, 1, rs_right)):
            arrived(ref.at[a, c, e, :, f], rs.at[u, n], rr.at[u, n])
        for e in range(2):
            part[a, c, y, e, :, f] = (
                part[a, c, y, e, :, f].astype(F32)
                + rs_left[a, c, e, :, f].astype(F32)
                + rs_right[a, c, e, :, f].astype(F32)
            ).astype(BF16)
        for o in range(1, NJ):
            jd = mate(o, 1)
            send(part.at[a, c, y, :, rows_of(jd), f], back.at[a, c, :, rows_of(j), f],
                 bs.at[u, o], br.at[u, o], z * NJ + jd, y)
        own[u] = pltpu.make_async_copy(
            part.at[a, c, y, :, rows_of(j), f], back.at[a, c, :, rows_of(j), f], bs.at[u, 0]
        )
        own[u].start()

    def combine(u):
        a, c, f = UNITS[u]
        for o in range(1, NJ):
            js = mate(o, -1)
            arrived(back.at[a, c, :, rows_of(js), f], bs.at[u, o], br.at[u, o])
        own[u].wait()
        width = f.stop - f.start
        got = back[a, c, :, :, f].reshape(EPL * ROWS, width)
        chosen = pick[c]
        span = slice(ZHALF * c, ZHALF * (c + 1))
        if a == 0:
            dots = dot_nt(got, dense[span].reshape(ZHALF * TOK, QW))
            dots = jnp.where(chosen > 0, dots, 0.0).reshape(EPL, ROWS, ZHALF * TOK)
            dots = jnp.sum(dots, axis=1)
            for i in range(ZHALF):
                for e in range(2):
                    dsend[ZHALF * c + i, e] = dots[e * NJ : (e + 1) * NJ, i * TOK : (i + 1) * TOK]
            got = (got.astype(F32) * prow[c]).astype(BF16)
        zsend[a, span, :, f] = dot_tn(chosen, got).astype(BF16).reshape(ZHALF, TOK, width)
        for i in range(ZHALF * c, ZHALF * (c + 1)):
            if i == 0:
                if a == 0:
                    dback[z] = dsend[0]
                continue
            zd = plane(i, 1)
            if a == 0:
                send(dsend.at[i], dback.at[z], zs.at[4, i], zr.at[4, i], zd * NJ + j, y)
            send(zsend.at[a, i, :, f], zback.at[a, i, :, f], ts.at[u, i], tr.at[u, i], zd * NJ + j, y)

    def finish(a, out):
        for u, (b, c, f) in enumerate(UNITS):
            if a == b:
                for i in range(max(1, ZHALF * c), ZHALF * (c + 1)):
                    arrived(zback.at[a, i, :, f], ts.at[u, i], tr.at[u, i])
        total = zsend[a, 0].astype(F32)
        for i in range(1, NZ):
            total = total + zback[a, i].astype(F32)
        out[...] = total.astype(BF16)

    def grads(e, carry):
        for q in range(NY):
            cols = slice(q * QW, (q + 1) * QW)
            for n, a, ref in ((0, 1, dwv), (1, 0, gwv), (2, 0, uwv)):
                ref[e, :, cols] = (dot_nn(acts[n, 0, e], rows[a, q, 0, e])
                                   + dot_nn(acts[n, 1, e], rows[a, q, 1, e])).astype(BF16)
        return carry

    gather_send(2, 0)
    gather_pass(2, 1, 2)
    gather_send(0, 0)
    routes(0)
    gather_pass(2, 3, 4)
    dispatch_cotangents(0)
    gather_pass(0, 1, 2)
    gather_send(1, 0)
    gather_pass(2, 5, 6)
    routes(1)
    gather_wait(0, 3)
    dispatch_tokens(0, 0)
    ring_send(1, 0)
    gather_wait(2, 7)
    dispatch_cotangents(1)
    gather_pass(1, 1, 2)
    gather_send(0, 3)
    gather_pass(0, 4)
    gather_wait(1, 3)
    dispatch_tokens(1, 0)
    gather_send(1, 3)
    gather_pass(1, 4)
    ring_forward(1, 0)
    ring_send(1, 1)
    gather_pass(0, 5, 6)
    gather_wait(0, 7)
    tokens_half(0, 0)
    dispatch_tokens(0, 1)
    gather_pass(1, 5, 6)
    gather_wait(1, 7)
    ring_end(1, 0)
    for load in wloads:
        load.wait()
    tokens_half(1, 0)
    dispatch_tokens(1, 1)
    ring_forward(1, 1)
    tokens_end(0)
    compute_out(0)
    scatter_first(0)
    scatter_plain(0)
    compute_dx(0)
    ring_end(1, 1)
    scatter_add(0)
    tokens_half(0, 1)
    tokens_half(1, 1)
    tokens_end(1)
    compute_out(1)
    scatter_first(1)
    scatter_plain(1)
    compute_dx(1)
    scatter_first(2)
    lax.fori_loop(0, 2, grads, 0)
    stores = [pltpu.make_async_copy(a, b, loc.at[5 + n])
              for n, (a, b) in enumerate(((gwv, ggate), (uwv, gup), (dwv, gdown)))]
    for store in stores:
        store.start()

    scatter_end(0)
    scatter_add(1)
    scatter_plain(2)
    combine(0)
    scatter_add(2)
    scatter_end(1)
    scatter_first(3)
    scatter_plain(3)
    combine(1)
    scatter_add(3)
    scatter_end(2)
    scatter_first(4)
    scatter_plain(4)
    combine(2)
    scatter_add(4)
    scatter_end(3)
    combine(3)
    scatter_end(4)

    for i in range(1, NZ):
        zo = plane(i, -1)
        arrived(dback.at[zo], zs.at[4, i], zr.at[4, i])
    every = dback[...].reshape(TOK, TOK)
    eid = lax.div(eio, EPL) * EPL + lax.rem(eio, NJ) * 2 + lax.rem(lax.div(eio, NJ), 2)
    for k in range(TOP):
        hit = eid == ids[k : k + 1, :]
        dy[0, k : k + 1, :] = jnp.sum(jnp.where(hit, every, 0.0), axis=0, keepdims=True)
    for n, h in ((1, right), (2, opp), (3, left)):
        send(dy.at[0], dy.at[n], dys.at[n], dyr.at[n], ex, h)
    finish(0, layer_out)
    combine(4)
    for n in range(1, NY):
        arrived(dy.at[n], dys.at[n], dyr.at[n])
    grad_probs = dy[0] + dy[1] + dy[2] + dy[3]
    grad_log[...] = probs * (grad_probs - jnp.sum(probs * grad_probs, axis=0, keepdims=True))
    finish(1, grad_tok)

    for store in stores:
        store.wait()
    for copy in sent:
        copy.wait_send()


def deliver_kernel(*refs):
    n = (len(refs) - 2) // 3
    src, dst, held = refs[:n], refs[n : 2 * n], refs[2 * n : 3 * n]
    ins = [pltpu.make_async_copy(src[i], held[i], refs[-2].at[i]) for i in range(n)]
    outs = [pltpu.make_async_copy(held[i], dst[i], refs[-1].at[i]) for i in range(n)]
    for copy in ins:
        copy.start()
    for copy_in, copy_out in zip(ins, outs):
        copy_in.wait()
        copy_out.start()
    for copy in outs:
        copy.wait()


def deliver(*arrays):
    n = len(arrays)
    spec = [pl.BlockSpec(memory_space=pl.ANY)] * n
    return pl.pallas_call(
        deliver_kernel,
        out_shape=tuple(jax.ShapeDtypeStruct(a.shape, a.dtype) for a in arrays),
        in_specs=spec,
        out_specs=tuple(spec),
        scratch_shapes=[pltpu.VMEM(a.shape, a.dtype) for a in arrays]
        + [pltpu.SemaphoreType.DMA((n,)), pltpu.SemaphoreType.DMA((n,))],
        compiler_params=pltpu.CompilerParams(vmem_limit_bytes=62 * 1024 * 1024),
    )(*arrays)


def body(tokens, logits, expert_ids, gate_weight, up_weight, down_weight, grad_out):
    any_spec = pl.BlockSpec(memory_space=pl.ANY)
    vmem = pl.BlockSpec(memory_space=pltpu.VMEM)
    half = ZHALF * CAP * NJ
    weight = jax.ShapeDtypeStruct(gate_weight.shape, BF16)
    quarter = jax.ShapeDtypeStruct((TOK, QW), BF16)
    layer_out, grad_tok, grad_log, ggate, gup, gdown = pl.pallas_call(
        kernel,
        out_shape=(quarter, quarter, jax.ShapeDtypeStruct((TOP, TOK), F32), weight, weight, weight),
        in_specs=[any_spec, vmem, vmem, any_spec, any_spec, any_spec, any_spec],
        out_specs=(vmem, vmem, vmem, any_spec, any_spec, any_spec),
        scratch_shapes=[
            pltpu.VMEM((NZ, TOK, QW), BF16),
            pltpu.VMEM((2, NZ, TOK, 2 * QW), BF16),
            pltpu.VMEM((2, TOK, TOK), F32),
            pltpu.VMEM((NZ, 2, EPL, TOK), F32),
            pltpu.VMEM((2, EPL * ROWS, ZHALF * TOK), BF16),
            pltpu.VMEM((2, EPL * ROWS, 1), F32),
            pltpu.VMEM((2, 2, half, QW), BF16),
            pltpu.VMEM((2, NY, 2, 2, half, QW), BF16),
            pltpu.VMEM(gate_weight.shape, BF16),
            pltpu.VMEM(gate_weight.shape, BF16),
            pltpu.VMEM(gate_weight.shape, BF16),
            pltpu.VMEM((3, 2, 2, gate_weight.shape[1], half), BF16),
            pltpu.VMEM((2, 2, half, gate_weight.shape[1]), BF16),
            pltpu.VMEM((2, 2, NY, 2, half, QW), BF16),
            pltpu.VMEM((2, 2, 2, half, QW), BF16),
            pltpu.VMEM((2, 2, 2, half, QW), BF16),
            pltpu.VMEM((2, 2, 2, half, QW), BF16),
            pltpu.VMEM((2, 2, 2, half, QW), BF16),
            pltpu.VMEM((2, NZ, TOK, QW), BF16),
            pltpu.VMEM((2, NZ, TOK, QW), BF16),
            pltpu.VMEM((NZ, 2, NJ, TOK), F32),
            pltpu.VMEM((NZ, 2, NJ, TOK), F32),
            pltpu.VMEM((NY, TOP, TOK), F32),
            pltpu.SemaphoreType.DMA((5, NZ + 1)),
            pltpu.SemaphoreType.DMA((5, NZ + 1)),
            pltpu.SemaphoreType.DMA((4, 2, NJ)),
            pltpu.SemaphoreType.DMA((4, 2, NJ)),
            pltpu.SemaphoreType.DMA((2, 6)),
            pltpu.SemaphoreType.DMA((2, 6)),
            pltpu.SemaphoreType.DMA((len(UNITS), 6)),
            pltpu.SemaphoreType.DMA((len(UNITS), 6)),
            pltpu.SemaphoreType.DMA((len(UNITS), NJ)),
            pltpu.SemaphoreType.DMA((len(UNITS), NJ)),
            pltpu.SemaphoreType.DMA((len(UNITS), NZ)),
            pltpu.SemaphoreType.DMA((len(UNITS), NZ)),
            pltpu.SemaphoreType.DMA((NY,)),
            pltpu.SemaphoreType.DMA((NY,)),
            pltpu.SemaphoreType.DMA((9,)),
            pltpu.SemaphoreType.DMA((4, 2)),
        ],
        compiler_params=pltpu.CompilerParams(
            collective_id=0, has_side_effects=True, vmem_limit_bytes=63 * 1024 * 1024
        ),
    )(tokens, expert_ids.T, logits.T, gate_weight, up_weight, down_weight, grad_out)
    layer_out, grad_tok, grad_log, ggate, gup, gdown = deliver(layer_out, grad_tok, grad_log, ggate, gup, gdown)
    return (layer_out, grad_tok, grad_log.T, ggate, gup, gdown)


def solution(mesh):
    placed = (
        P("expert", None),
        P("expert", None),
        P("expert", None),
        P("expert", "hid", None),
        P("expert", "hid", None),
        P("expert", "hid", None),
        P("expert", "hid"),
    )
    return jax.shard_map(
        body,
        mesh=mesh,
        in_specs=placed,
        out_specs=(
            P("expert", "hid"),
            P("expert", "hid"),
            P("expert", None),
            P("expert", "hid", None),
            P("expert", "hid", None),
            P("expert", "hid", None),
        ),
        check_vma=False,
    )
```
